128 devices in a mesh: row: 8 (over x_lo, y), col: 16 (over z, x_hi, core).
Axes of the slice: x: 4 (x_hi: 2, x_lo: 2; x = x_hi * 2 + x_lo), y: 4, z: 4, core: 2. Of those that a mesh axis runs over, the one named last changes fastest.
Arguments:
- slab: float32 [4096, 4, 2048], P(('row', 'col')), may hold values from -0.75 to 0.75
- occ_energy: float32 [4], replicated, may hold values from -1.2 to -0.4
- vir_energy: float32 [2048], replicated, may hold values from 0.3 to 3.4
Outputs:
- amplitudes: float32 [6, 2048, 2048], P(None, 'row', 'col')
- pair_energy: float32 [6], replicated
The draws below stay inside these ranges and needn't reach their ends.
All inputs are finite; a program needn't handle non-finite values.
Results may differ from the reference program's by a relative error of at most 0.0001.
Values sent between devices are 32-bit elements; how exact they have to be, the bound alone decides.
A program may use at most 128 MiB of HBM per device.

```python
import jax
import jax.numpy as jnp
from jax import lax

NAUX = 4096
NVIR = 2048
OCC = 4


def draw_vir_energy(key, part):
    key = jax.random.fold_in(key, 7)
    ramp = 0.3 + 2.7 * jnp.arange(NVIR, dtype=jnp.float32) / NVIR
    jitter = jax.random.uniform(key, (NVIR,), jnp.float32, 0.0, 0.2)
    return ramp + jitter


def block_scale(rng, shape, pieces, smallest, high):
    def one(axis_at, blocks):
        heights = jax.random.uniform(jax.random.fold_in(jax.random.fold_in(rng, 6), axis_at), (blocks,), jnp.float32, smallest / len(pieces), high / len(pieces))
        return jnp.repeat(jnp.exp(heights), shape[axis_at] // blocks).reshape((-1,) + (1,) * (len(shape) - axis_at - 1))

    gain = one(*pieces[0])
    for cut in pieces[1:]:
        gain = gain * one(*cut)
    return gain


def scatter_about(stream_key, extent, scale, bound, cuts=(), held_as=jnp.bfloat16):
    factor_of = block_scale(stream_key, extent, cuts, -0.22, 0.18) if cuts else 1.0
    result = jax.random.normal(stream_key, extent, jnp.float32) * scale * factor_of
    return jnp.minimum(jnp.maximum(result, -bound), bound).astype(held_as)


def setup_inputs(seed: int = 0) -> dict:
    streams_of = jax.random.split(jax.random.key(seed), 4)
    return {
        "slab": scatter_about(streams_of[0], (NAUX, OCC, NVIR), 0.125, 0.75, ((0, 128),), jnp.float32),
        "occ_energy": jnp.clip(jax.random.uniform(streams_of[1], (OCC,), jnp.float32, -1.2, -0.4), -1.2, -0.4),
        "vir_energy": draw_vir_energy(jax.random.fold_in(streams_of[3], 71), 0),
    }


pair_list = [(0, 1), (0, 2), (0, 3), (1, 2), (1, 3), (2, 3)]


def reference(slab, occ_energy, vir_energy):
    amps = []
    energies = []
    for first, second in pair_list:
        direct = jnp.dot(slab[:, first, :].T, slab[:, second, :], precision=lax.Precision.HIGHEST, preferred_element_type=jnp.float32)
        denom = occ_energy[first] + occ_energy[second] - vir_energy[:, None] - vir_energy[None, :]
        amp = direct / denom
        amps.append(amp)
        energies.append(2.0 * jnp.sum(amp * (2.0 * direct - direct.T)) / (NVIR * NVIR))
    return jnp.stack(amps), jnp.stack(energies)
```

```python
import jax
import jax.numpy as jnp
from jax import lax
from jax.experimental import pallas as pl
from jax.experimental.pallas import tpu as pltpu
from jax.sharding import PartitionSpec as P

F32, BF16 = jnp.float32, jnp.bfloat16
NQ = 32
NV = 2048
SEQ = [(0, 0, 2), (0, 1, 1), (1, 0, 4), (1, 1, 3), (0, 2, 0), (2, 0, 5)]
PAIRS = [(0, 1), (0, 2), (0, 3), (1, 2), (1, 3), (2, 3)]


def kernel(
    slab, occ, vir, amps, energy,
    send_l, send_r, left, right, lt_hi, lt_lo, r_hi, r_lo,
    part, part_in, x_in, dfin, t_in, vir_a, e_acc, e_col, e_row,
    a_s, a_r, g_s, g_r, f_s, f_r, d_s, d_r, x_s, x_r, t_s, t_r, e1_s, e1_r, e2_s, e2_r,
):
    row = lax.axis_index("row")
    col = lax.axis_index("col")
    x_lo, y = row // 4, row % 4
    z, x_hi, core = col // 4, (col // 2) % 2, col % 2
    colchip = col // 2

    def at_y(d):
        return {"row": x_lo * 4 + (y + d) % 4}

    def at_z(d):
        return {"col": ((z + d) % 4) * 4 + x_hi * 2 + core}

    def at_x(d):
        xx = (x_hi * 2 + x_lo + d) % 4
        return {"row": (xx % 2) * 4 + y, "col": (z * 2 + xx // 2) * 2 + core}

    sibling = {"col": colchip * 2 + 1 - core}

    def partner(h):
        return {"row": colchip, "col": row * 2 + h}

    bar = pltpu.get_barrier_semaphore()
    for d in range(1, 8):
        pl.semaphore_signal(bar, inc=1, device_id={"row": (row + d) % 8})
    for d in range(1, 16):
        pl.semaphore_signal(bar, inc=1, device_id={"col": (col + d) % 16})
    pl.semaphore_signal(
        bar, inc=1, device_id={"row": (1 - x_lo) * 4 + y, "col": (z * 2 + 1 - x_hi) * 2 + core}
    )

    @pl.when(row != colchip)
    def _():
        for h in range(2):
            pl.semaphore_signal(bar, inc=1, device_id=partner(h))

    def stage(o):
        v = slab[:, o, :]
        for k in range(4):
            send_l[o, k, :, 0:256] = v[:, k * 256 : k * 256 + 256]
            send_l[o, k, :, 256:512] = v[:, 1024 + k * 256 : 1280 + k * 256]
        w = slab[:, 3 - o, :]
        for k in range(4):
            for c in range(2):
                for h in range(2):
                    b = k * 512 + h * 256 + c * 128
                    send_r[o, k, :, c * 256 + h * 128 : c * 256 + h * 128 + 128] = w[:, b : b + 128]
        left[o, z, y] = send_l[o, y]
        right[o, y, z] = send_r[o, z]

    stage(0)
    pl.semaphore_wait(bar, jnp.where(row == colchip, 23, 25))

    started = []

    def copy(src, dst, ssem, rsem, to):
        cp = pltpu.make_async_remote_copy(src, dst, ssem, rsem, device_id=to)
        cp.start()
        started.append(cp)
        return cp

    scatter, gather, onward = {}, {}, {}

    def post_scatter(o):
        for d in (1, 3, 2):
            ky, kz = (y + d) % 4, (z + d) % 4
            scatter[o, 0, d] = copy(
                send_l.at[o, ky], left.at[o, z, y], a_s.at[0, o, d - 1], a_r.at[0, o, d - 1], at_y(d)
            )
            scatter[o, 1, d] = copy(
                send_r.at[o, kz], right.at[o, y, z], a_s.at[1, o, d - 1], a_r.at[1, o, d - 1], at_z(d)
            )

    def post_gather(o, d):
        ky, kz = (y - d) % 4, (z - d) % 4
        for way, step in ((0, 1), (1, 3)):
            gather[o, 0, way, d] = copy(
                left.at[o, z, ky], left.at[o, z, ky], g_s.at[0, o, way, d], g_r.at[0, o, way, d], at_z(step)
            )
            gather[o, 1, way, d] = copy(
                right.at[o, y, kz], right.at[o, y, kz], g_s.at[1, o, way, d], g_r.at[1, o, way, d], at_y(step)
            )

    def rest_gather(o):
        for d in (1, 3, 2):
            scatter[o, 0, d].wait_recv()
            scatter[o, 1, d].wait_recv()
            post_gather(o, d)

    def forward(o):
        for way, step, half in ((0, 1, 0), (1, 3, 2)):
            for side in range(2):
                for d in range(4):
                    gather[o, side, way, d].wait_recv()
            kz, ky = (z - step) % 4, (y - step) % 4
            onward[o, 0, way] = copy(
                left.at[o, kz, pl.ds(half, 2)], left.at[o, kz, pl.ds(half, 2)],
                f_s.at[0, o, way], f_r.at[0, o, way], at_z(step),
            )
            onward[o, 1, way] = copy(
                right.at[o, ky, pl.ds(half, 2)], right.at[o, ky, pl.ds(half, 2)],
                f_s.at[1, o, way], f_r.at[1, o, way], at_y(step),
            )

    def prepare(o):
        for way in range(2):
            onward[o, 0, way].wait_recv()
            onward[o, 1, way].wait_recv()
        for k in range(4):
            v = left[o, k].reshape(128, 512).T
            hi = v.astype(BF16)
            lt_hi[o, :, k * 128 : k * 128 + 128] = hi
            lt_lo[o, :, k * 128 : k * 128 + 128] = (v - hi.astype(F32)).astype(BF16)
        for kz in range(4):
            for ky in range(4):
                w = right[o, ky, kz]
                hi = w.astype(BF16)
                lo = (w - hi.astype(F32)).astype(BF16)
                q = kz * 128 + ky * 32
                for h in range(2):
                    r_hi[o, h, q : q + 32, :] = hi[:, h * 256 : h * 256 + 256]
                    r_lo[o, h, q : q + 32, :] = lo[:, h * 256 : h * 256 + 256]

    def multiply(s, which, half):
        lo_, ro_, _ = SEQ[s]

        @pl.loop(0, 2)
        def _(ab):
            rows = pl.ds(pl.multiple_of(ab * 256, 256), 256)
            hi = lt_hi[lo_, rows, :]
            acc = jnp.dot(hi, r_hi[ro_, half], preferred_element_type=F32)
            acc += jnp.dot(hi, r_lo[ro_, half], preferred_element_type=F32)
            acc += jnp.dot(lt_lo[lo_, rows, :], r_hi[ro_, half], preferred_element_type=F32)
            part[s, which, ab] = acc[:, 0:128]
            part[s, which, 2 + ab] = acc[:, 128:256]

    exchanged, along_x = {}, {}
    me_x = x_hi * 2 + x_lo

    def compute(s):
        multiply(s, 0, 1 - core)
        exchanged[s] = copy(part.at[s, 0], part_in.at[s], d_s.at[s], d_r.at[s], sibling)
        multiply(s, 1, core)

    def reduce(s):
        exchanged[s].wait_recv()
        part[s, 1] = part[s, 1] + part_in[s]
        for d in (1, 3, 2):
            along_x[s, d] = copy(
                part.at[s, 1, (me_x + d) % 4], x_in.at[s, d - 1], x_s.at[s, d - 1], x_r.at[s, d - 1], at_x(d)
            )

    def swap(s, h):
        return pltpu.make_async_remote_copy(
            dfin.at[s, pl.ds(pl.multiple_of(h * 128, 128), 128)], t_in.at[s, core], t_s.at[s, h], t_r.at[s, core],
            device_id=partner(h),
        )

    def swap_sibling(s):
        return pltpu.make_async_remote_copy(
            dfin.at[s, pl.ds(pl.multiple_of((1 - core) * 128, 128), 128)], t_in.at[s, core],
            t_s.at[s, 0], t_r.at[s, core], device_id=sibling,
        )

    def sends(s):
        return row < colchip if s % 2 == 0 else row > colchip

    def receives(s):
        return row > colchip if s % 2 == 0 else row < colchip

    vir_b = vir[pl.ds(col, 1), :]

    def finish(s):
        for d in range(1, 4):
            along_x[s, d].wait_recv()
        p = SEQ[s][2]
        i, j = PAIRS[p]
        total = (part[s, 1, me_x] + x_in[s, 0]) + (x_in[s, 1] + x_in[s, 2])
        dfin[s] = total

        @pl.when(sends(s))
        def _():
            for h in range(2):
                swap(s, h).start()

        @pl.when(row == colchip)
        def _():
            swap_sibling(s).start()
            t_in[s, core] = dfin[s, pl.ds(pl.multiple_of(core * 128, 128), 128), :]

        amp = total / (((occ[i] + occ[j]) - vir_a[...]) - vir_b)
        amps[p] = amp
        e_acc[p] = jnp.sum((2.0 * (amp * total)).reshape(32, 8, 128), axis=0)

    def energy_swapped(s, weight):
        p = SEQ[s][2]
        prod = amps[p, 0:128] * t_in[s, 0].T + amps[p, 128:256] * t_in[s, 1].T
        e_acc[p] = e_acc[p] - weight * jnp.sum(prod.reshape(16, 8, 128), axis=0)

    def swapped(s):
        @pl.when(receives(s))
        def _():
            for h in range(2):
                pltpu.make_async_remote_copy(
                    t_in.at[s, h], t_in.at[s, h], t_s.at[s, h], t_r.at[s, h], device_id=sibling
                ).wait_recv()
            energy_swapped(s, 2.0)

        @pl.when(row == colchip)
        def _():
            pltpu.make_async_remote_copy(
                t_in.at[s, 1 - core], t_in.at[s, 1 - core], t_s.at[s, 0], t_r.at[s, 1 - core], device_id=sibling
            ).wait_recv()
            energy_swapped(s, 1.0)
            swap_sibling(s).wait_send()

        @pl.when(sends(s))
        def _():
            for h in range(2):
                swap(s, h).wait_send()

    post_scatter(0)
    post_gather(0, 0)
    stage(1)
    rest_gather(0)
    post_scatter(1)
    post_gather(1, 0)
    stage(2)
    for h in range(2):
        vir_a[h * 128 : h * 128 + 128, :] = jnp.broadcast_to(vir[pl.ds(row * 2 + h, 1), :], (128, 128)).T
    forward(0)
    rest_gather(1)
    post_scatter(2)
    post_gather(2, 0)
    prepare(0)
    compute(0)
    forward(1)
    rest_gather(2)
    reduce(0)
    prepare(1)
    compute(1)
    compute(2)
    reduce(1)
    compute(3)
    reduce(2)
    reduce(3)
    forward(2)
    finish(0)
    swapped(0)
    prepare(2)
    compute(4)
    compute(5)
    reduce(4)
    reduce(5)
    for s in range(1, 6):
        finish(s)
    for s in range(1, 6):
        swapped(s)

    e_tile = jnp.concatenate(
        [jnp.sum(e_acc[p], axis=0, keepdims=True) for p in range(6)] + [jnp.zeros((2, 128), F32)], axis=0
    )
    e_col[col] = e_tile
    hops = []
    for d in range(1, 16):
        hops.append(copy(e_col.at[col], e_col.at[col], e1_s.at[d - 1], e1_r.at[d - 1], {"col": (col + d) % 16}))
    for cp in hops:
        cp.wait_recv()
    e_row[row] = jnp.sum(e_col[...], axis=0)
    hops = []
    for d in range(1, 8):
        hops.append(copy(e_row.at[row], e_row.at[row], e2_s.at[d - 1], e2_r.at[d - 1], {"row": (row + d) % 8}))
    for cp in hops:
        cp.wait_recv()
    whole = jnp.sum(jnp.sum(e_row[...], axis=0), axis=1, keepdims=True)
    energy[...] = jnp.broadcast_to(whole * (2.0 / (NV * NV)), (8, 128))
    for cp in started:
        cp.wait_send()


def local(slab, occ_energy, vir_energy):
    dma = pltpu.SemaphoreType.DMA
    vmem = pltpu.VMEM
    both = lambda *shape: [dma(shape), dma(shape)]
    amps, energy = pl.pallas_call(
        kernel,
        out_shape=(
            jax.ShapeDtypeStruct((6, 256, 128), F32),
            jax.ShapeDtypeStruct((8, 128), F32),
        ),
        in_specs=[
            pl.BlockSpec(memory_space=vmem),
            pl.BlockSpec(memory_space=pltpu.SMEM),
            pl.BlockSpec(memory_space=vmem),
        ],
        out_specs=(pl.BlockSpec(memory_space=vmem), pl.BlockSpec(memory_space=vmem)),
        scratch_shapes=[
            vmem((3, 4, NQ, 512), F32),
            vmem((3, 4, NQ, 512), F32),
            vmem((3, 4, 4, NQ, 512), F32),
            vmem((3, 4, 4, NQ, 512), F32),
            vmem((3, 512, 512), BF16),
            vmem((3, 512, 512), BF16),
            vmem((3, 2, 512, 256), BF16),
            vmem((3, 2, 512, 256), BF16),
            vmem((6, 2, 4, 256, 128), F32),
            vmem((6, 4, 256, 128), F32),
            vmem((6, 3, 256, 128), F32),
            vmem((6, 256, 128), F32),
            vmem((6, 2, 128, 128), F32),
            vmem((256, 128), F32),
            vmem((6, 8, 128), F32),
            vmem((16, 8, 128), F32),
            vmem((8, 8, 128), F32),
            *both(2, 3, 3),
            *both(2, 3, 2, 4),
            *both(2, 3, 2),
            *both(6),
            *both(6, 3),
            *both(6, 2),
            *both(15),
            *both(7),
        ],
        compiler_params=pltpu.CompilerParams(
            collective_id=0, has_side_effects=True, vmem_limit_bytes=48 * 2**20
        ),
        name="pairs",
    )(slab, occ_energy, vir_energy.reshape(16, 128))
    return amps, energy[:6, 0]


def solution(mesh):
    return jax.shard_map(
        local,
        mesh=mesh,
        in_specs=(P(("row", "col"), None, None), P(), P()),
        out_specs=(P(None, "row", "col"), P()),
        check_vma=False,
    )
```

```python
import jax
import jax.numpy as jnp
from jax import lax
from jax.experimental import pallas as pl
from jax.experimental.pallas import tpu as pltpu
from jax.sharding import PartitionSpec as P

F32, BF16 = jnp.float32, jnp.bfloat16
NQ = 32
NV = 2048
SEQ = [(0, 0, 2), (0, 1, 1), (1, 0, 4), (1, 1, 3), (0, 2, 0), (2, 0, 5)]
PAIRS = [(0, 1), (0, 2), (0, 3), (1, 2), (1, 3), (2, 3)]


def kernel(
    slab, occ, vir, amps, energy,
    send_l, send_r, left, right, lt_hi, lt_lo, r_hi, r_lo,
    part, part_in, x_in, x_via, dfin, t_in, vir_a, e_acc, e_col, e_row,
    a_s, a_r, g_s, g_r, f_s, f_r, d_s, d_r, x_s, x_r, t_s, t_r, e1_s, e1_r, e2_s, e2_r,
):
    row = lax.axis_index("row")
    col = lax.axis_index("col")
    x_lo, y = row // 4, row % 4
    z, x_hi, core = col // 4, (col // 2) % 2, col % 2
    colchip = col // 2

    def at_y(d):
        return {"row": x_lo * 4 + (y + d) % 4}

    def at_z(d):
        return {"col": ((z + d) % 4) * 4 + x_hi * 2 + core}

    def at_x(d):
        xx = (x_hi * 2 + x_lo + d) % 4
        return {"row": (xx % 2) * 4 + y, "col": (z * 2 + xx // 2) * 2 + core}

    sibling = {"col": colchip * 2 + 1 - core}

    def partner(h):
        return {"row": colchip, "col": row * 2 + h}

    bar = pltpu.get_barrier_semaphore()
    for d in range(1, 8):
        pl.semaphore_signal(bar, inc=1, device_id={"row": (row + d) % 8})
    for d in range(1, 16):
        pl.semaphore_signal(bar, inc=1, device_id={"col": (col + d) % 16})
    pl.semaphore_signal(
        bar, inc=1, device_id={"row": (1 - x_lo) * 4 + y, "col": (z * 2 + 1 - x_hi) * 2 + core}
    )

    @pl.when(row != colchip)
    def _():
        for h in range(2):
            pl.semaphore_signal(bar, inc=1, device_id=partner(h))

    def stage(o):
        v = slab[:, o, :]
        for k in range(4):
            send_l[o, k, :, 0:256] = v[:, k * 256 : k * 256 + 256]
            send_l[o, k, :, 256:512] = v[:, 1024 + k * 256 : 1280 + k * 256]
        w = slab[:, 3 - o, :]
        for k in range(4):
            for c in range(2):
                for h in range(2):
                    b = k * 512 + h * 256 + c * 128
                    send_r[o, k, :, c * 256 + h * 128 : c * 256 + h * 128 + 128] = w[:, b : b + 128]
        left[o, z, y] = send_l[o, y]
        right[o, y, z] = send_r[o, z]

    stage(0)
    pl.semaphore_wait(bar, jnp.where(row == colchip, 23, 25))

    started = []

    def copy(src, dst, ssem, rsem, to):
        cp = pltpu.make_async_remote_copy(src, dst, ssem, rsem, device_id=to)
        cp.start()
        started.append(cp)
        return cp

    scatter, gather, onward = {}, {}, {}

    def post_scatter(o):
        for d in (1, 3, 2):
            ky, kz = (y + d) % 4, (z + d) % 4
            scatter[o, 0, d] = copy(
                send_l.at[o, ky], left.at[o, z, y], a_s.at[0, o, d - 1], a_r.at[0, o, d - 1], at_y(d)
            )
            scatter[o, 1, d] = copy(
                send_r.at[o, kz], right.at[o, y, z], a_s.at[1, o, d - 1], a_r.at[1, o, d - 1], at_z(d)
            )

    def post_gather(o, d):
        ky, kz = (y - d) % 4, (z - d) % 4
        for way, step in ((0, 1), (1, 3)):
            gather[o, 0, way, d] = copy(
                left.at[o, z, ky], left.at[o, z, ky], g_s.at[0, o, way, d], g_r.at[0, o, way, d], at_z(step)
            )
            gather[o, 1, way, d] = copy(
                right.at[o, y, kz], right.at[o, y, kz], g_s.at[1, o, way, d], g_r.at[1, o, way, d], at_y(step)
            )

    def rest_gather(o):
        for d in (1, 3, 2):
            scatter[o, 0, d].wait_recv()
            scatter[o, 1, d].wait_recv()
            post_gather(o, d)

    def forward(o, d):
        way, step = (0, 1) if d % 2 == 0 else (1, 3)
        kz, ky = (z - step) % 4, (y - step) % 4
        jy, jz = (y - d) % 4, (z - d) % 4
        gather[o, 0, way, d].wait_recv()
        onward[o, 0, d] = copy(
            left.at[o, kz, jy], left.at[o, kz, jy], f_s.at[0, o, d], f_r.at[0, o, d], at_z(step)
        )
        gather[o, 1, way, d].wait_recv()
        onward[o, 1, d] = copy(
            right.at[o, ky, jz], right.at[o, ky, jz], f_s.at[1, o, d], f_r.at[1, o, d], at_y(step)
        )

    def prepare(o):
        for side in range(2):
            for d in range(4):
                gather[o, side, 1 - (d % 2), d].wait_recv()
                onward[o, side, d].wait_recv()
        for k in range(4):
            v = left[o, k].reshape(128, 512).T
            hi = v.astype(BF16)
            lt_hi[o, :, k * 128 : k * 128 + 128] = hi
            lt_lo[o, :, k * 128 : k * 128 + 128] = (v - hi.astype(F32)).astype(BF16)
        for kz in range(4):
            for ky in range(4):
                w = right[o, ky, kz]
                hi = w.astype(BF16)
                lo = (w - hi.astype(F32)).astype(BF16)
                q = kz * 128 + ky * 32
                for h in range(2):
                    r_hi[o, h, q : q + 32, :] = hi[:, h * 256 : h * 256 + 256]
                    r_lo[o, h, q : q + 32, :] = lo[:, h * 256 : h * 256 + 256]

    def multiply(s, which, half):
        lo_, ro_, _ = SEQ[s]

        @pl.loop(0, 2)
        def _(ab):
            rows = pl.ds(pl.multiple_of(ab * 256, 256), 256)
            hi = lt_hi[lo_, rows, :]
            acc = jnp.dot(hi, r_hi[ro_, half], preferred_element_type=F32)
            acc += jnp.dot(hi, r_lo[ro_, half], preferred_element_type=F32)
            acc += jnp.dot(lt_lo[lo_, rows, :], r_hi[ro_, half], preferred_element_type=F32)
            part[s, which, ab] = acc[:, 0:128]
            part[s, which, 2 + ab] = acc[:, 128:256]

    exchanged, along_x = {}, {}
    me_x = x_hi * 2 + x_lo

    def compute(s):
        multiply(s, 0, 1 - core)
        exchanged[s] = copy(part.at[s, 0], part_in.at[s], d_s.at[s], d_r.at[s], sibling)
        multiply(s, 1, core)

    up_x, down_x, far_x = (me_x + 1) % 4, (me_x + 3) % 4, (me_x + 2) % 4
    low, high = pl.ds(0, 128), pl.ds(128, 128)

    def reduce(s):
        exchanged[s].wait_recv()
        part[s, 1] = part[s, 1] + part_in[s]
        mine = part.at[s, 1]
        along_x[s, 0] = copy(mine.at[far_x, low], x_via.at[s, 0], x_s.at[s, 0], x_r.at[s, 0], at_x(1))
        along_x[s, 1] = copy(mine.at[far_x, high], x_via.at[s, 1], x_s.at[s, 1], x_r.at[s, 1], at_x(3))
        along_x[s, 2] = copy(mine.at[up_x, high], x_in.at[s, 0, high], x_s.at[s, 2], x_r.at[s, 2], at_x(1))
        along_x[s, 3] = copy(mine.at[down_x, low], x_in.at[s, 1, low], x_s.at[s, 3], x_r.at[s, 3], at_x(3))

    def reduce_on(s):
        mine = part.at[s, 1]
        along_x[s, 0].wait_recv()
        part[s, 1, up_x, 0:128] = part[s, 1, up_x, 0:128] + x_via[s, 0]
        along_x[s, 4] = copy(mine.at[up_x, low], x_in.at[s, 0, low], x_s.at[s, 4], x_r.at[s, 4], at_x(1))
        along_x[s, 1].wait_recv()
        part[s, 1, down_x, 128:256] = part[s, 1, down_x, 128:256] + x_via[s, 1]
        along_x[s, 5] = copy(mine.at[down_x, high], x_in.at[s, 1, high], x_s.at[s, 5], x_r.at[s, 5], at_x(3))

    def swap(s, h):
        return pltpu.make_async_remote_copy(
            dfin.at[s, pl.ds(pl.multiple_of(h * 128, 128), 128)], t_in.at[s, core], t_s.at[s, h], t_r.at[s, core],
            device_id=partner(h),
        )

    def swap_sibling(s):
        return pltpu.make_async_remote_copy(
            dfin.at[s, pl.ds(pl.multiple_of((1 - core) * 128, 128), 128)], t_in.at[s, core],
            t_s.at[s, 0], t_r.at[s, core], device_id=sibling,
        )

    def sends(s):
        return row < colchip if s % 2 == 0 else row > colchip

    def receives(s):
        return row > colchip if s % 2 == 0 else row < colchip

    vir_b = vir[pl.ds(col, 1), :]

    def finish(s):
        for k in range(2, 6):
            along_x[s, k].wait_recv()
        p = SEQ[s][2]
        i, j = PAIRS[p]
        total = part[s, 1, me_x] + (x_in[s, 0] + x_in[s, 1])
        dfin[s] = total

        @pl.when(sends(s))
        def _():
            for h in range(2):
                swap(s, h).start()

        @pl.when(row == colchip)
        def _():
            swap_sibling(s).start()
            t_in[s, core] = dfin[s, pl.ds(pl.multiple_of(core * 128, 128), 128), :]

        amp = total / (((occ[i] + occ[j]) - vir_a[...]) - vir_b)
        amps[p] = amp
        e_acc[p] = jnp.sum((2.0 * (amp * total)).reshape(32, 8, 128), axis=0)

    def energy_swapped(s, weight):
        p = SEQ[s][2]
        prod = amps[p, 0:128] * t_in[s, 0].T + amps[p, 128:256] * t_in[s, 1].T
        e_acc[p] = e_acc[p] - weight * jnp.sum(prod.reshape(16, 8, 128), axis=0)

    def swapped(s):
        @pl.when(receives(s))
        def _():
            for h in range(2):
                pltpu.make_async_remote_copy(
                    t_in.at[s, h], t_in.at[s, h], t_s.at[s, h], t_r.at[s, h], device_id=sibling
                ).wait_recv()
            energy_swapped(s, 2.0)

        @pl.when(row == colchip)
        def _():
            pltpu.make_async_remote_copy(
                t_in.at[s, 1 - core], t_in.at[s, 1 - core], t_s.at[s, 0], t_r.at[s, 1 - core], device_id=sibling
            ).wait_recv()
            energy_swapped(s, 1.0)
            swap_sibling(s).wait_send()

        @pl.when(sends(s))
        def _():
            for h in range(2):
                swap(s, h).wait_send()

    def forward_rest(o):
        for d in (1, 3, 2):
            forward(o, d)

    post_scatter(0)
    post_gather(0, 0)
    stage(1)
    rest_gather(0)
    forward(0, 0)
    post_scatter(1)
    post_gather(1, 0)
    stage(2)
    for h in range(2):
        vir_a[h * 128 : h * 128 + 128, :] = jnp.broadcast_to(vir[pl.ds(row * 2 + h, 1), :], (128, 128)).T
    forward_rest(0)
    rest_gather(1)
    forward(1, 0)
    post_scatter(2)
    post_gather(2, 0)
    prepare(0)
    compute(0)
    reduce(0)
    forward_rest(1)
    reduce_on(0)
    rest_gather(2)
    forward(2, 0)
    prepare(1)
    compute(1)
    compute(2)
    reduce(1)
    finish(0)
    compute(3)
    reduce(2)
    reduce_on(1)
    reduce(3)
    reduce_on(2)
    forward_rest(2)
    reduce_on(3)
    finish(1)
    finish(2)
    finish(3)
    prepare(2)
    compute(4)
    compute(5)
    reduce(4)
    reduce(5)
    swapped(0)
    reduce_on(4)
    reduce_on(5)
    for s in range(1, 4):
        swapped(s)
    finish(4)
    finish(5)
    swapped(4)
    swapped(5)

    e_tile = jnp.concatenate(
        [jnp.sum(e_acc[p], axis=0, keepdims=True) for p in range(6)] + [jnp.zeros((2, 128), F32)], axis=0
    )
    e_col[col] = e_tile
    hops = []
    for d in range(1, 16):
        hops.append(copy(e_col.at[col], e_col.at[col], e1_s.at[d - 1], e1_r.at[d - 1], {"col": (col + d) % 16}))
    for cp in hops:
        cp.wait_recv()
    e_row[row] = jnp.sum(e_col[...], axis=0)
    hops = []
    for d in range(1, 8):
        hops.append(copy(e_row.at[row], e_row.at[row], e2_s.at[d - 1], e2_r.at[d - 1], {"row": (row + d) % 8}))
    for cp in hops:
        cp.wait_recv()
    whole = jnp.sum(jnp.sum(e_row[...], axis=0), axis=1, keepdims=True)
    energy[...] = jnp.broadcast_to(whole * (2.0 / (NV * NV)), (8, 128))
    for cp in started:
        cp.wait_send()


def local(slab, occ_energy, vir_energy):
    dma = pltpu.SemaphoreType.DMA
    vmem = pltpu.VMEM
    both = lambda *shape: [dma(shape), dma(shape)]
    amps, energy = pl.pallas_call(
        kernel,
        out_shape=(
            jax.ShapeDtypeStruct((6, 256, 128), F32),
            jax.ShapeDtypeStruct((8, 128), F32),
        ),
        in_specs=[
            pl.BlockSpec(memory_space=vmem),
            pl.BlockSpec(memory_space=pltpu.SMEM),
            pl.BlockSpec(memory_space=vmem),
        ],
        out_specs=(pl.BlockSpec(memory_space=vmem), pl.BlockSpec(memory_space=vmem)),
        scratch_shapes=[
            vmem((3, 4, NQ, 512), F32),
            vmem((3, 4, NQ, 512), F32),
            vmem((3, 4, 4, NQ, 512), F32),
            vmem((3, 4, 4, NQ, 512), F32),
            vmem((3, 512, 512), BF16),
            vmem((3, 512, 512), BF16),
            vmem((3, 2, 512, 256), BF16),
            vmem((3, 2, 512, 256), BF16),
            vmem((6, 2, 4, 256, 128), F32),
            vmem((6, 4, 256, 128), F32),
            vmem((6, 2, 256, 128), F32),
            vmem((6, 2, 128, 128), F32),
            vmem((6, 256, 128), F32),
            vmem((6, 2, 128, 128), F32),
            vmem((256, 128), F32),
            vmem((6, 8, 128), F32),
            vmem((16, 8, 128), F32),
            vmem((8, 8, 128), F32),
            *both(2, 3, 3),
            *both(2, 3, 2, 4),
            *both(2, 3, 4),
            *both(6),
            *both(6, 6),
            *both(6, 2),
            *both(15),
            *both(7),
        ],
        compiler_params=pltpu.CompilerParams(
            collective_id=0, has_side_effects=True, vmem_limit_bytes=48 * 2**20
        ),
        name="pairs",
    )(slab, occ_energy, vir_energy.reshape(16, 128))
    return amps, energy[:6, 0]


def solution(mesh):
    return jax.shard_map(
        local,
        mesh=mesh,
        in_specs=(P(("row", "col"), None, None), P(), P()),
        out_specs=(P(None, "row", "col"), P()),
        check_vma=False,
    )
```

```python
import jax
import jax.numpy as jnp
from jax import lax
from jax.experimental import pallas as pl
from jax.experimental.pallas import tpu as pltpu
from jax.sharding import PartitionSpec as P

F32, BF16 = jnp.float32, jnp.bfloat16
NQ = 32
NV = 2048
SEQ = [(0, 0, 2), (0, 1, 1), (1, 0, 4), (1, 1, 3), (0, 2, 0), (2, 0, 5)]
PAIRS = [(0, 1), (0, 2), (0, 3), (1, 2), (1, 3), (2, 3)]


def kernel(
    slab, occ, vir, amps, energy,
    send_l, send_r, left, right, lt_hi, lt_lo, r_hi, r_lo,
    part, part_in, x_in, x_via, dfin, t_in, via, vir_a, e_acc, e_col, e_row,
    a_s, a_r, g_s, g_r, f_s, f_r, d_s, d_r, x_s, x_r, t_s, t_r, v_s, v_r, e1_s, e1_r, e2_s, e2_r,
):
    row = lax.axis_index("row")
    col = lax.axis_index("col")
    x_lo, y = row // 4, row % 4
    z, x_hi, core = col // 4, (col // 2) % 2, col % 2
    colchip = col // 2

    def at_y(d):
        return {"row": x_lo * 4 + (y + d) % 4}

    def at_z(d):
        return {"col": ((z + d) % 4) * 4 + x_hi * 2 + core}

    def at_x(d):
        xx = (x_hi * 2 + x_lo + d) % 4
        return {"row": (xx % 2) * 4 + y, "col": (z * 2 + xx // 2) * 2 + core}

    sibling = {"col": colchip * 2 + 1 - core}

    def partner(h):
        return {"row": colchip, "col": row * 2 + h}

    bar = pltpu.get_barrier_semaphore()
    for d in range(1, 8):
        pl.semaphore_signal(bar, inc=1, device_id={"row": (row + d) % 8})
    for d in range(1, 16):
        pl.semaphore_signal(bar, inc=1, device_id={"col": (col + d) % 16})
    pl.semaphore_signal(
        bar, inc=1, device_id={"row": (1 - x_lo) * 4 + y, "col": (z * 2 + 1 - x_hi) * 2 + core}
    )

    @pl.when(row != colchip)
    def _():
        for h in range(2):
            pl.semaphore_signal(bar, inc=1, device_id=partner(h))

    me_x = x_hi * 2 + x_lo
    relay_row = x_lo * 4 + colchip % 4
    relay_chip = (row // 2) * 2 + x_hi
    to_x = (row % 2) * 2 + colchip // 4
    hop_x = (to_x - me_x + 4) % 4
    by_relay = (hop_x != 0) & ((relay_row != row) | (relay_chip != colchip))

    def source(k):
        xx = (me_x + k) % 4
        y_s = (z % 2) * 2 + xx // 2
        z_s = (xx % 2) * 2 + y // 2
        there = (x_hi == y % 2) & (x_lo == z // 2) & ((y_s != y) | (z_s != z))
        return x_lo * 4 + y_s, z_s * 2 + x_hi, there

    for k in range(1, 4):
        row_s, chip_s, there = source(k)

        @pl.when(there)
        def _():
            for h in range(2):
                pl.semaphore_signal(bar, inc=1, device_id={"row": row_s, "col": chip_s * 2 + h})

    def stage(o):
        v = slab[:, o, :]
        for k in range(4):
            send_l[o, k, :, 0:256] = v[:, k * 256 : k * 256 + 256]
            send_l[o, k, :, 256:512] = v[:, 1024 + k * 256 : 1280 + k * 256]
        w = slab[:, 3 - o, :]
        for k in range(4):
            for c in range(2):
                for h in range(2):
                    b = k * 512 + h * 256 + c * 128
                    send_r[o, k, :, c * 256 + h * 128 : c * 256 + h * 128 + 128] = w[:, b : b + 128]
        left[o, z, y] = send_l[o, y]
        right[o, y, z] = send_r[o, z]

    stage(0)
    pl.semaphore_wait(bar, 23 + jnp.where(row == colchip, 0, 2) + jnp.where(by_relay, 2, 0))

    started = []

    def copy(src, dst, ssem, rsem, to):
        cp = pltpu.make_async_remote_copy(src, dst, ssem, rsem, device_id=to)
        cp.start()
        started.append(cp)
        return cp

    scatter, gather, onward = {}, {}, {}

    def post_scatter(o):
        for d in (1, 3, 2):
            ky, kz = (y + d) % 4, (z + d) % 4
            scatter[o, 0, d] = copy(
                send_l.at[o, ky], left.at[o, z, y], a_s.at[0, o, d - 1], a_r.at[0, o, d - 1], at_y(d)
            )
            scatter[o, 1, d] = copy(
                send_r.at[o, kz], right.at[o, y, z], a_s.at[1, o, d - 1], a_r.at[1, o, d - 1], at_z(d)
            )

    def post_gather(o, d):
        ky, kz = (y - d) % 4, (z - d) % 4
        for way, step in ((0, 1), (1, 3)):
            gather[o, 0, way, d] = copy(
                left.at[o, z, ky], left.at[o, z, ky], g_s.at[0, o, way, d], g_r.at[0, o, way, d], at_z(step)
            )
            gather[o, 1, way, d] = copy(
                right.at[o, y, kz], right.at[o, y, kz], g_s.at[1, o, way, d], g_r.at[1, o, way, d], at_y(step)
            )

    def rest_gather(o):
        for d in (1, 3, 2):
            scatter[o, 0, d].wait_recv()
            scatter[o, 1, d].wait_recv()
            post_gather(o, d)

    def forward(o, d):
        way, step = (0, 1) if d % 2 == 0 else (1, 3)
        kz, ky = (z - step) % 4, (y - step) % 4
        jy, jz = (y - d) % 4, (z - d) % 4
        gather[o, 0, way, d].wait_recv()
        onward[o, 0, d] = copy(
            left.at[o, kz, jy], left.at[o, kz, jy], f_s.at[0, o, d], f_r.at[0, o, d], at_z(step)
        )
        gather[o, 1, way, d].wait_recv()
        onward[o, 1, d] = copy(
            right.at[o, ky, jz], right.at[o, ky, jz], f_s.at[1, o, d], f_r.at[1, o, d], at_y(step)
        )

    def prepare(o):
        for side in range(2):
            for d in range(4):
                gather[o, side, 1 - (d % 2), d].wait_recv()
                onward[o, side, d].wait_recv()
        for k in range(4):
            v = left[o, k].reshape(128, 512).T
            hi = v.astype(BF16)
            lt_hi[o, :, k * 128 : k * 128 + 128] = hi
            lt_lo[o, :, k * 128 : k * 128 + 128] = (v - hi.astype(F32)).astype(BF16)
        for kz in range(4):
            for ky in range(4):
                w = right[o, ky, kz]
                hi = w.astype(BF16)
                lo = (w - hi.astype(F32)).astype(BF16)
                q = kz * 128 + ky * 32
                for h in range(2):
                    r_hi[o, h, q : q + 32, :] = hi[:, h * 256 : h * 256 + 256]
                    r_lo[o, h, q : q + 32, :] = lo[:, h * 256 : h * 256 + 256]

    def multiply(s, which, half):
        lo_, ro_, _ = SEQ[s]

        @pl.loop(0, 2)
        def _(ab):
            rows = pl.ds(pl.multiple_of(ab * 256, 256), 256)
            hi = lt_hi[lo_, rows, :]
            acc = jnp.dot(hi, r_hi[ro_, half], preferred_element_type=F32)
            acc += jnp.dot(hi, r_lo[ro_, half], preferred_element_type=F32)
            acc += jnp.dot(lt_lo[lo_, rows, :], r_hi[ro_, half], preferred_element_type=F32)
            part[s, which, ab] = acc[:, 0:128]
            part[s, which, 2 + ab] = acc[:, 128:256]

    exchanged, along_x = {}, {}

    def compute(s):
        multiply(s, 0, 1 - core)
        exchanged[s] = copy(part.at[s, 0], part_in.at[s], d_s.at[s], d_r.at[s], sibling)
        multiply(s, 1, core)

    up_x, down_x, far_x = (me_x + 1) % 4, (me_x + 3) % 4, (me_x + 2) % 4
    low, high = pl.ds(0, 128), pl.ds(128, 128)

    def reduce(s):
        exchanged[s].wait_recv()
        part[s, 1] = part[s, 1] + part_in[s]
        mine = part.at[s, 1]
        along_x[s, 0] = copy(mine.at[far_x, low], x_via.at[s, 0], x_s.at[s, 0], x_r.at[s, 0], at_x(1))
        along_x[s, 1] = copy(mine.at[far_x, high], x_via.at[s, 1], x_s.at[s, 1], x_r.at[s, 1], at_x(3))
        along_x[s, 2] = copy(mine.at[up_x, high], x_in.at[s, 0, high], x_s.at[s, 2], x_r.at[s, 2], at_x(1))
        along_x[s, 3] = copy(mine.at[down_x, low], x_in.at[s, 1, low], x_s.at[s, 3], x_r.at[s, 3], at_x(3))

    def reduce_on(s):
        mine = part.at[s, 1]
        along_x[s, 0].wait_recv()
        part[s, 1, up_x, 0:128] = part[s, 1, up_x, 0:128] + x_via[s, 0]
        along_x[s, 4] = copy(mine.at[up_x, low], x_in.at[s, 0, low], x_s.at[s, 4], x_r.at[s, 4], at_x(1))
        along_x[s, 1].wait_recv()
        part[s, 1, down_x, 128:256] = part[s, 1, down_x, 128:256] + x_via[s, 1]
        along_x[s, 5] = copy(mine.at[down_x, high], x_in.at[s, 1, high], x_s.at[s, 5], x_r.at[s, 5], at_x(3))

    def swap(s, h, part_no):
        rows = pl.ds(pl.multiple_of(h * 128 + part_no * 64, 64), 64)
        return pltpu.make_async_remote_copy(
            dfin.at[s, rows], t_in.at[s, core, pl.ds(part_no * 64, 64)],
            t_s.at[s, h, part_no], t_r.at[s, core, part_no], device_id=partner(h),
        )

    def swap_by_relay(s, h):
        rows = pl.ds(pl.multiple_of(h * 128 + 64, 64), 64)
        return pltpu.make_async_remote_copy(
            dfin.at[s, rows], via.at[s, hop_x - 1, core], t_s.at[s, h, 1], v_r.at[s, hop_x - 1, core],
            device_id={"row": relay_row, "col": relay_chip * 2 + h},
        )

    def onto(s, k, c):
        row_s, chip_s, _ = source(k)
        return pltpu.make_async_remote_copy(
            via.at[s, k - 1, c], t_in.at[s, c, pl.ds(64, 64)], v_s.at[s, k - 1, c], t_r.at[s, c, 1],
            device_id={"row": chip_s, "col": row_s * 2 + core},
        )

    def relays(s, k):
        row_s, chip_s, there = source(k)
        return there & (row_s < chip_s if s % 2 == 0 else row_s > chip_s)

    def relay(s):
        for k in range(1, 4):

            @pl.when(relays(s, k))
            def _():
                for c in range(2):
                    pltpu.make_async_remote_copy(
                        via.at[s, k - 1, c], via.at[s, k - 1, c], v_s.at[s, k - 1, c], v_r.at[s, k - 1, c], device_id=sibling
                    ).wait_recv()
                    onto(s, k, c).start()

    def swap_sibling(s):
        return pltpu.make_async_remote_copy(
            dfin.at[s, pl.ds(pl.multiple_of((1 - core) * 128, 128), 128)], t_in.at[s, core],
            t_s.at[s, 0, 0], t_r.at[s, core, 0], device_id=sibling,
        )

    def sends(s):
        return row < colchip if s % 2 == 0 else row > colchip

    def receives(s):
        return row > colchip if s % 2 == 0 else row < colchip

    vir_b = vir[pl.ds(col, 1), :]

    def finish(s):
        for k in range(2, 6):
            along_x[s, k].wait_recv()
        p = SEQ[s][2]
        i, j = PAIRS[p]
        total = part[s, 1, me_x] + (x_in[s, 0] + x_in[s, 1])
        dfin[s] = total

        amp = total / (((occ[i] + occ[j]) - vir_a[...]) - vir_b)
        amps[p] = amp
        e_acc[p] = jnp.sum((2.0 * (amp * total)).reshape(32, 8, 128), axis=0)

    def swap_start(s):
        @pl.when(sends(s))
        def _():
            for h in range(2):
                swap(s, h, 0).start()

        @pl.when(sends(s) & by_relay)
        def _():
            for h in range(2):
                swap_by_relay(s, h).start()

        @pl.when(sends(s) & jnp.logical_not(by_relay))
        def _():
            for h in range(2):
                swap(s, h, 1).start()

        @pl.when(row == colchip)
        def _():
            swap_sibling(s).start()
            t_in[s, core] = dfin[s, pl.ds(pl.multiple_of(core * 128, 128), 128), :]

    def swap_sent(s):
        @pl.when(sends(s))
        def _():
            for h in range(2):
                for n in range(2):
                    swap(s, h, n).wait_send()

        @pl.when(row == colchip)
        def _():
            swap_sibling(s).wait_send()

        for k in range(1, 4):

            @pl.when(relays(s, k))
            def _():
                for c in range(2):
                    onto(s, k, c).wait_send()

    def energy_swapped(s, weight):
        p = SEQ[s][2]
        prod = amps[p, 0:128] * t_in[s, 0].T + amps[p, 128:256] * t_in[s, 1].T
        e_acc[p] = e_acc[p] - weight * jnp.sum(prod.reshape(16, 8, 128), axis=0)

    def swapped(s):
        @pl.when(receives(s))
        def _():
            for h in range(2):
                for n in range(2):
                    half = t_in.at[s, h, pl.ds(n * 64, 64)]
                    pltpu.make_async_remote_copy(
                        half, half, t_s.at[s, h, n], t_r.at[s, h, n], device_id=sibling
                    ).wait_recv()
            energy_swapped(s, 2.0)

        @pl.when(row == colchip)
        def _():
            pltpu.make_async_remote_copy(
                t_in.at[s, 1 - core], t_in.at[s, 1 - core], t_s.at[s, 0, 0], t_r.at[s, 1 - core, 0], device_id=sibling
            ).wait_recv()
            energy_swapped(s, 1.0)

    def forward_rest(o):
        for d in (1, 3, 2):
            forward(o, d)

    post_scatter(0)
    post_gather(0, 0)
    stage(1)
    rest_gather(0)
    forward(0, 0)
    post_scatter(1)
    post_gather(1, 0)
    stage(2)
    for h in range(2):
        vir_a[h * 128 : h * 128 + 128, :] = jnp.broadcast_to(vir[pl.ds(row * 2 + h, 1), :], (128, 128)).T
    forward_rest(0)
    rest_gather(1)
    forward(1, 0)
    post_scatter(2)
    post_gather(2, 0)
    prepare(0)
    compute(0)
    reduce(0)
    forward_rest(1)
    reduce_on(0)
    rest_gather(2)
    forward(2, 0)
    finish(0)
    prepare(1)
    compute(1)
    compute(2)
    reduce(1)
    compute(3)
    reduce(2)
    reduce(3)
    forward_rest(2)
    swap_start(0)
    reduce_on(1)
    reduce_on(2)
    reduce_on(3)
    prepare(2)
    compute(4)
    compute(5)
    reduce(4)
    reduce(5)
    for s in range(1, 4):
        finish(s)
        swap_start(s)
        relay(s - 1)
    reduce_on(4)
    swapped(0)
    reduce_on(5)
    swapped(1)
    relay(3)
    swapped(2)
    finish(4)
    swap_start(4)
    finish(5)
    swap_start(5)
    swapped(3)
    relay(4)
    relay(5)
    swapped(4)
    swapped(5)

    e_tile = jnp.concatenate(
        [jnp.sum(e_acc[p], axis=0, keepdims=True) for p in range(6)] + [jnp.zeros((2, 128), F32)], axis=0
    )
    e_col[col] = e_tile
    hops = []
    for d in range(1, 16):
        hops.append(copy(e_col.at[col], e_col.at[col], e1_s.at[d - 1], e1_r.at[d - 1], {"col": (col + d) % 16}))
    for cp in started[: -len(hops)]:
        cp.wait_send()
    del started[: -len(hops)]
    for s in range(6):
        swap_sent(s)
    for cp in hops:
        cp.wait_recv()
    e_row[row] = jnp.sum(e_col[...], axis=0)
    hops = []
    for d in range(1, 8):
        hops.append(copy(e_row.at[row], e_row.at[row], e2_s.at[d - 1], e2_r.at[d - 1], {"row": (row + d) % 8}))
    for cp in hops:
        cp.wait_recv()
    whole = jnp.sum(jnp.sum(e_row[...], axis=0), axis=1, keepdims=True)
    energy[...] = jnp.broadcast_to(whole * (2.0 / (NV * NV)), (8, 128))
    for cp in started:
        cp.wait_send()


def local(slab, occ_energy, vir_energy):
    dma = pltpu.SemaphoreType.DMA
    vmem = pltpu.VMEM
    both = lambda *shape: [dma(shape), dma(shape)]
    amps, energy = pl.pallas_call(
        kernel,
        out_shape=(
            jax.ShapeDtypeStruct((6, 256, 128), F32),
            jax.ShapeDtypeStruct((8, 128), F32),
        ),
        in_specs=[
            pl.BlockSpec(memory_space=vmem),
            pl.BlockSpec(memory_space=pltpu.SMEM),
            pl.BlockSpec(memory_space=vmem),
        ],
        out_specs=(pl.BlockSpec(memory_space=vmem), pl.BlockSpec(memory_space=vmem)),
        scratch_shapes=[
            vmem((3, 4, NQ, 512), F32),
            vmem((3, 4, NQ, 512), F32),
            vmem((3, 4, 4, NQ, 512), F32),
            vmem((3, 4, 4, NQ, 512), F32),
            vmem((3, 512, 512), BF16),
            vmem((3, 512, 512), BF16),
            vmem((3, 2, 512, 256), BF16),
            vmem((3, 2, 512, 256), BF16),
            vmem((6, 2, 4, 256, 128), F32),
            vmem((6, 4, 256, 128), F32),
            vmem((6, 2, 256, 128), F32),
            vmem((6, 2, 128, 128), F32),
            vmem((6, 256, 128), F32),
            vmem((6, 2, 128, 128), F32),
            vmem((6, 3, 2, 64, 128), F32),
            vmem((256, 128), F32),
            vmem((6, 8, 128), F32),
            vmem((16, 8, 128), F32),
            vmem((8, 8, 128), F32),
            *both(2, 3, 3),
            *both(2, 3, 2, 4),
            *both(2, 3, 4),
            *both(6),
            *both(6, 6),
            *both(6, 2, 2),
            *both(6, 3, 2),
            *both(15),
            *both(7),
        ],
        compiler_params=pltpu.CompilerParams(
            collective_id=0, has_side_effects=True, vmem_limit_bytes=48 * 2**20
        ),
        name="pairs",
    )(slab, occ_energy, vir_energy.reshape(16, 128))
    return amps, energy[:6, 0]


def solution(mesh):
    return jax.shard_map(
        local,
        mesh=mesh,
        in_specs=(P(("row", "col"), None, None), P(), P()),
        out_specs=(P(None, "row", "col"), P()),
        check_vma=False,
    )
```

```python
import jax
import jax.numpy as jnp
from jax import lax
from jax.experimental import pallas as pl
from jax.experimental.pallas import tpu as pltpu
from jax.sharding import PartitionSpec as P

F32, BF16 = jnp.float32, jnp.bfloat16
NQ = 32
NV = 2048
SEQ = [(0, 0, 2), (0, 1, 1), (1, 0, 4), (1, 1, 3), (0, 2, 0), (2, 0, 5)]
PAIRS = [(0, 1), (0, 2), (0, 3), (1, 2), (1, 3), (2, 3)]


def kernel(
    slab_hbm, occ_hbm, vir_hbm, amps_hbm, energy,
    slab, occ, vir, amps,
    send_l, send_r, left, right, lt_hi, lt_lo, r_hi, r_lo,
    part, part_in, x_in, x_via, dfin, t_in, via, vir_a, e_acc, e_col, e_row,
    a_s, a_r, g_s, g_r, u_r, f_s, d_s, d_r, x_s, x_r, t_s, t_r, v_s, v_r, e1_s, e1_r, e2_s, e2_r, i_s, o_s,
):
    row = lax.axis_index("row")
    col = lax.axis_index("col")
    x_lo, y = row // 4, row % 4
    z, x_hi, core = col // 4, (col // 2) % 2, col % 2
    colchip = col // 2

    def at_y(d):
        return {"row": x_lo * 4 + (y + d) % 4}

    def at_z(d):
        return {"col": ((z + d) % 4) * 4 + x_hi * 2 + core}

    def at_x(d):
        xx = (x_hi * 2 + x_lo + d) % 4
        return {"row": (xx % 2) * 4 + y, "col": (z * 2 + xx // 2) * 2 + core}

    sibling = {"col": colchip * 2 + 1 - core}

    def partner(h):
        return {"row": colchip, "col": row * 2 + h}

    inputs = [
        pltpu.make_async_copy(src, dst, i_s.at[n])
        for n, (src, dst) in enumerate([(slab_hbm, slab), (occ_hbm, occ), (vir_hbm, vir)])
    ]
    for cp in inputs:
        cp.start()
    bar = pltpu.get_barrier_semaphore()
    for d in range(1, 8):
        pl.semaphore_signal(bar, inc=1, device_id={"row": (row + d) % 8})
    for d in range(1, 16):
        pl.semaphore_signal(bar, inc=1, device_id={"col": (col + d) % 16})
    pl.semaphore_signal(
        bar, inc=1, device_id={"row": (1 - x_lo) * 4 + y, "col": (z * 2 + 1 - x_hi) * 2 + core}
    )

    @pl.when(row != colchip)
    def _():
        for h in range(2):
            pl.semaphore_signal(bar, inc=1, device_id=partner(h))

    me_x = x_hi * 2 + x_lo
    relay_row = x_lo * 4 + colchip % 4
    relay_chip = (row // 2) * 2 + x_hi
    to_x = (row % 2) * 2 + colchip // 4
    hop_x = (to_x - me_x + 4) % 4
    by_relay = (hop_x != 0) & ((relay_row != row) | (relay_chip != colchip))

    def source(k):
        xx = (me_x + k) % 4
        y_s = (z % 2) * 2 + xx // 2
        z_s = (xx % 2) * 2 + y // 2
        there = (x_hi == y % 2) & (x_lo == z // 2) & ((y_s != y) | (z_s != z))
        return x_lo * 4 + y_s, z_s * 2 + x_hi, there

    for k in range(1, 4):
        row_s, chip_s, there = source(k)

        @pl.when(there)
        def _():
            for h in range(2):
                pl.semaphore_signal(bar, inc=1, device_id={"row": row_s, "col": chip_s * 2 + h})

    def stage(o):
        v = slab[:, o, :]
        for k in range(4):
            send_l[o, k, :, 0:256] = v[:, k * 256 : k * 256 + 256]
            send_l[o, k, :, 256:512] = v[:, 1024 + k * 256 : 1280 + k * 256]
        w = slab[:, 3 - o, :]
        for k in range(4):
            for c in range(2):
                for h in range(2):
                    b = k * 512 + h * 256 + c * 128
                    send_r[o, k, :, c * 256 + h * 128 : c * 256 + h * 128 + 128] = w[:, b : b + 128]
        left[o, z, y] = send_l[o, y]
        right[o, y, z] = send_r[o, z]

    for cp in inputs:
        cp.wait()
    stage(0)
    pl.semaphore_wait(bar, 23 + jnp.where(row == colchip, 0, 2) + jnp.where(by_relay, 2, 0))

    def copy(src, dst, ssem, rsem, to):
        cp = pltpu.make_async_remote_copy(src, dst, ssem, rsem, device_id=to)
        cp.start()
        return cp

    def took(sem, like):
        pltpu.make_async_copy(like, like, sem).wait()

    scatter, gather = {}, {}

    def post_scatter(o):
        for d in (1, 3, 2):
            ky, kz = (y + d) % 4, (z + d) % 4
            scatter[o, 0, d] = copy(
                send_l.at[o, ky], left.at[o, z, y], a_s, a_r.at[0, o, d - 1], at_y(d)
            )
            scatter[o, 1, d] = copy(
                send_r.at[o, kz], right.at[o, y, z], a_s, a_r.at[1, o, d - 1], at_z(d)
            )

    def post_gather(o, d):
        ky, kz = (y - d) % 4, (z - d) % 4
        for way, step in ((0, 1), (1, 3)):
            sems = [g_r.at[side, o, d] if way == d % 2 else u_r.at[side, o] for side in range(2)]
            gather[o, 0, way, d] = copy(left.at[o, z, ky], left.at[o, z, ky], g_s, sems[0], at_z(step))
            gather[o, 1, way, d] = copy(right.at[o, y, kz], right.at[o, y, kz], g_s, sems[1], at_y(step))

    def rest_gather(o):
        for d in (1, 3, 2):
            scatter[o, 0, d].wait_recv()
            scatter[o, 1, d].wait_recv()
            post_gather(o, d)

    def forward(o, d):
        way, step = (0, 1) if d % 2 == 0 else (1, 3)
        kz, ky = (z - step) % 4, (y - step) % 4
        jy, jz = (y - d) % 4, (z - d) % 4
        gather[o, 0, way, d].wait_recv()
        copy(left.at[o, kz, jy], left.at[o, kz, jy], f_s, u_r.at[0, o], at_z(step))
        gather[o, 1, way, d].wait_recv()
        copy(right.at[o, ky, jz], right.at[o, ky, jz], f_s, u_r.at[1, o], at_y(step))

    def prepare(o):
        took(u_r.at[0, o], left.at[o, 0:2])
        took(u_r.at[1, o], right.at[o, 0:2])
        for k in range(4):
            v = left[o, k].reshape(128, 512).T
            hi = v.astype(BF16)
            lt_hi[o, :, k * 128 : k * 128 + 128] = hi
            lt_lo[o, :, k * 128 : k * 128 + 128] = (v - hi.astype(F32)).astype(BF16)
        for kz in range(4):
            for ky in range(4):
                w = right[o, ky, kz]
                hi = w.astype(BF16)
                lo = (w - hi.astype(F32)).astype(BF16)
                q = kz * 128 + ky * 32
                for h in range(2):
                    r_hi[o, h, q : q + 32, :] = hi[:, h * 256 : h * 256 + 256]
                    r_lo[o, h, q : q + 32, :] = lo[:, h * 256 : h * 256 + 256]

    def multiply(s, which, half):
        lo_, ro_, _ = SEQ[s]

        @pl.loop(0, 2)
        def _(ab):
            rows = pl.ds(pl.multiple_of(ab * 256, 256), 256)
            hi = lt_hi[lo_, rows, :]
            acc = jnp.dot(hi, r_hi[ro_, half], preferred_element_type=F32)
            acc += jnp.dot(hi, r_lo[ro_, half], preferred_element_type=F32)
            acc += jnp.dot(lt_lo[lo_, rows, :], r_hi[ro_, half], preferred_element_type=F32)
            part[s, which, ab] = acc[:, 0:128]
            part[s, which, 2 + ab] = acc[:, 128:256]

    exchanged, along_x = {}, {}

    def compute(s):
        multiply(s, 0, 1 - core)
        exchanged[s] = copy(part.at[s, 0], part_in.at[s], d_s, d_r.at[s], sibling)
        multiply(s, 1, core)

    up_x, down_x, far_x = (me_x + 1) % 4, (me_x + 3) % 4, (me_x + 2) % 4
    low, high = pl.ds(0, 128), pl.ds(128, 128)

    def reduce(s):
        exchanged[s].wait_recv()
        part[s, 1] = part[s, 1] + part_in[s]
        mine = part.at[s, 1]
        along_x[s, 0] = copy(mine.at[far_x, low], x_via.at[s, 0], x_s, x_r.at[s, 0], at_x(1))
        along_x[s, 1] = copy(mine.at[far_x, high], x_via.at[s, 1], x_s, x_r.at[s, 1], at_x(3))
        copy(mine.at[up_x, high], x_in.at[s, 0, high], x_s, x_r.at[s, 2], at_x(1))
        copy(mine.at[down_x, low], x_in.at[s, 1, low], x_s, x_r.at[s, 2], at_x(3))

    def reduce_on(s):
        mine = part.at[s, 1]
        along_x[s, 0].wait_recv()
        part[s, 1, up_x, 0:128] = part[s, 1, up_x, 0:128] + x_via[s, 0]
        copy(mine.at[up_x, low], x_in.at[s, 0, low], x_s, x_r.at[s, 2], at_x(1))
        along_x[s, 1].wait_recv()
        part[s, 1, down_x, 128:256] = part[s, 1, down_x, 128:256] + x_via[s, 1]
        copy(mine.at[down_x, high], x_in.at[s, 1, high], x_s, x_r.at[s, 2], at_x(3))

    def swap(s, h, part_no):
        rows = pl.ds(pl.multiple_of(h * 128 + part_no * 64, 64), 64)
        return pltpu.make_async_remote_copy(
            dfin.at[s, rows], t_in.at[s, core, pl.ds(part_no * 64, 64)],
            t_s.at[s], t_r.at[s], device_id=partner(h),
        )

    def swap_by_relay(s, h):
        rows = pl.ds(pl.multiple_of(h * 128 + 64, 64), 64)
        return pltpu.make_async_remote_copy(
            dfin.at[s, rows], via.at[s, hop_x - 1, core], t_s.at[s], v_r.at[s, hop_x - 1],
            device_id={"row": relay_row, "col": relay_chip * 2 + h},
        )

    def onto(s, k, c):
        row_s, chip_s, _ = source(k)
        return pltpu.make_async_remote_copy(
            via.at[s, k - 1, c], t_in.at[s, c, pl.ds(64, 64)], v_s.at[s, k - 1], t_r.at[s],
            device_id={"row": chip_s, "col": row_s * 2 + core},
        )

    def relays(s, k):
        row_s, chip_s, there = source(k)
        return there & (row_s < chip_s if s % 2 == 0 else row_s > chip_s)

    def relay(s):
        for k in range(1, 4):

            @pl.when(relays(s, k))
            def _():
                took(v_r.at[s, k - 1], via.at[s, k - 1])
                for c in range(2):
                    onto(s, k, c).start()

    def swap_sibling(s):
        return pltpu.make_async_remote_copy(
            dfin.at[s, pl.ds(pl.multiple_of((1 - core) * 128, 128), 128)], t_in.at[s, core],
            t_s.at[s], t_r.at[s], device_id=sibling,
        )

    def sends(s):
        return row < colchip if s % 2 == 0 else row > colchip

    def receives(s):
        return row > colchip if s % 2 == 0 else row < colchip

    written = []
    vir_b = vir[pl.ds(col, 1), :]

    def finish(s):
        took(x_r.at[s, 2], x_in.at[s])
        p = SEQ[s][2]
        i, j = PAIRS[p]
        total = part[s, 1, me_x] + (x_in[s, 0] + x_in[s, 1])
        dfin[s] = total

        amp = total / (((occ[i] + occ[j]) - vir_a[...]) - vir_b)
        amps[p] = amp
        written.append(pltpu.make_async_copy(amps.at[p], amps_hbm.at[p], o_s.at[p]))
        written[-1].start()
        e_acc[p] = jnp.sum((2.0 * (amp * total)).reshape(32, 8, 128), axis=0)

    def swap_start(s):
        @pl.when(sends(s))
        def _():
            for h in range(2):
                swap(s, h, 0).start()

        @pl.when(sends(s) & by_relay)
        def _():
            for h in range(2):
                swap_by_relay(s, h).start()

        @pl.when(sends(s) & jnp.logical_not(by_relay))
        def _():
            for h in range(2):
                swap(s, h, 1).start()

        @pl.when(row == colchip)
        def _():
            swap_sibling(s).start()
            t_in[s, core] = dfin[s, pl.ds(pl.multiple_of(core * 128, 128), 128), :]

    def swap_sent(s):
        @pl.when(sends(s))
        def _():
            took(t_s.at[s], dfin.at[s])

        @pl.when(row == colchip)
        def _():
            took(t_s.at[s], t_in.at[s, 0])

        for k in range(1, 4):

            @pl.when(relays(s, k))
            def _():
                took(v_s.at[s, k - 1], via.at[s, k - 1])

    def energy_swapped(s, weight):
        p = SEQ[s][2]
        prod = amps[p, 0:128] * t_in[s, 0].T + amps[p, 128:256] * t_in[s, 1].T
        e_acc[p] = e_acc[p] - weight * jnp.sum(prod.reshape(16, 8, 128), axis=0)

    def swapped(s):
        @pl.when(receives(s))
        def _():
            took(t_r.at[s], t_in.at[s])
            energy_swapped(s, 2.0)

        @pl.when(row == colchip)
        def _():
            took(t_r.at[s], t_in.at[s, 1 - core])
            energy_swapped(s, 1.0)

    def forward_rest(o):
        for d in (1, 3, 2):
            forward(o, d)

    post_scatter(0)
    post_gather(0, 0)
    stage(1)
    rest_gather(0)
    forward(0, 0)
    post_scatter(1)
    post_gather(1, 0)
    stage(2)
    for h in range(2):
        vir_a[h * 128 : h * 128 + 128, :] = jnp.broadcast_to(vir[pl.ds(row * 2 + h, 1), :], (128, 128)).T
    forward_rest(0)
    rest_gather(1)
    forward(1, 0)
    post_scatter(2)
    post_gather(2, 0)
    prepare(0)
    compute(0)
    reduce(0)
    forward_rest(1)
    reduce_on(0)
    rest_gather(2)
    forward(2, 0)
    finish(0)
    prepare(1)
    compute(1)
    compute(2)
    reduce(1)
    compute(3)
    reduce(2)
    reduce(3)
    forward_rest(2)
    swap_start(0)
    reduce_on(1)
    reduce_on(2)
    reduce_on(3)
    prepare(2)
    compute(4)
    compute(5)
    reduce(4)
    reduce(5)
    for s in range(1, 4):
        finish(s)
        swap_start(s)
        relay(s - 1)
    reduce_on(4)
    swapped(0)
    reduce_on(5)
    swapped(1)
    relay(3)
    swapped(2)
    finish(4)
    swap_start(4)
    finish(5)
    swap_start(5)
    swapped(3)
    relay(4)
    relay(5)
    swapped(4)
    swapped(5)

    e_tile = jnp.concatenate(
        [jnp.sum(e_acc[p], axis=0, keepdims=True) for p in range(6)] + [jnp.zeros((2, 128), F32)], axis=0
    )
    e_col[col] = e_tile
    for d in range(1, 16):
        copy(e_col.at[col], e_col.at[col], e1_s, e1_r, {"col": (col + d) % 16})
    took(a_s, left.at[:, 0:3, 0:2])
    took(g_s, left)
    took(f_s, left.at[:, 0:2])
    took(d_s, part_in)
    took(x_s, part.at[:, 0, 0:3])
    for s in range(6):
        swap_sent(s)
    took(e1_r, e_col.at[0:15])
    e_row[row] = jnp.sum(e_col[...], axis=0)
    for d in range(1, 8):
        copy(e_row.at[row], e_row.at[row], e2_s, e2_r, {"row": (row + d) % 8})
    took(e1_s, e_col.at[0:15])
    took(e2_r, e_row.at[0:7])
    whole = jnp.sum(jnp.sum(e_row[...], axis=0), axis=1, keepdims=True)
    energy[...] = jnp.broadcast_to(whole * (2.0 / (NV * NV)), (8, 128))
    took(e2_s, e_row.at[0:7])
    for cp in written:
        cp.wait()


def local(slab, occ_energy, vir_energy):
    dma = pltpu.SemaphoreType.DMA
    vmem = pltpu.VMEM
    amps, energy = pl.pallas_call(
        kernel,
        out_shape=(
            jax.ShapeDtypeStruct((6, 256, 128), F32),
            jax.ShapeDtypeStruct((8, 128), F32),
        ),
        in_specs=[pl.BlockSpec(memory_space=pltpu.HBM)] * 3,
        out_specs=(pl.BlockSpec(memory_space=pltpu.HBM), pl.BlockSpec(memory_space=vmem)),
        scratch_shapes=[
            vmem((NQ, 4, NV), F32),
            pltpu.SMEM((4,), F32),
            vmem((16, 128), F32),
            vmem((6, 256, 128), F32),
            vmem((3, 4, NQ, 512), F32),
            vmem((3, 4, NQ, 512), F32),
            vmem((3, 4, 4, NQ, 512), F32),
            vmem((3, 4, 4, NQ, 512), F32),
            vmem((3, 512, 512), BF16),
            vmem((3, 512, 512), BF16),
            vmem((3, 2, 512, 256), BF16),
            vmem((3, 2, 512, 256), BF16),
            vmem((6, 2, 4, 256, 128), F32),
            vmem((6, 4, 256, 128), F32),
            vmem((6, 2, 256, 128), F32),
            vmem((6, 2, 128, 128), F32),
            vmem((6, 256, 128), F32),
            vmem((6, 2, 128, 128), F32),
            vmem((6, 3, 2, 64, 128), F32),
            vmem((256, 128), F32),
            vmem((6, 8, 128), F32),
            vmem((16, 8, 128), F32),
            vmem((8, 8, 128), F32),
            dma,
            dma((2, 3, 3)),
            dma,
            dma((2, 3, 4)),
            dma((2, 3)),
            dma,
            dma,
            dma((6,)),
            dma,
            dma((6, 3)),
            dma((6,)),
            dma((6,)),
            dma((6, 3)),
            dma((6, 3)),
            dma,
            dma,
            dma,
            dma,
            dma((3,)),
            dma((6,)),
        ],
        compiler_params=pltpu.CompilerParams(
            collective_id=0, has_side_effects=True, vmem_limit_bytes=60 * 2**20
        ),
        name="pairs",
    )(slab, occ_energy, vir_energy.reshape(16, 128))
    return amps, energy[:6, 0]


def solution(mesh):
    return jax.shard_map(
        local,
        mesh=mesh,
        in_specs=(P(("row", "col"), None, None), P(), P()),
        out_specs=(P(None, "row", "col"), P()),
        check_vma=False,
    )
```

```python
import jax
import jax.numpy as jnp
from jax import lax
from jax.experimental import pallas as pl
from jax.experimental.pallas import tpu as pltpu
from jax.sharding import PartitionSpec as P

F32, BF16 = jnp.float32, jnp.bfloat16
NQ = 32
NV = 2048
SEQ = [(0, 0, 2), (0, 1, 1), (1, 0, 4), (1, 1, 3), (0, 2, 0), (2, 0, 5)]
PAIRS = [(0, 1), (0, 2), (0, 3), (1, 2), (1, 3), (2, 3)]


def kernel(
    slab_hbm, occ_hbm, vir_hbm, amps_hbm, energy,
    slab, occ, vir, amps,
    send_l, send_r, left, right, lt_hi, lt_lo, r_hi, r_lo,
    part, part_in, x_in, x_via, dfin, t_in, via, vir_a, e_acc, e_col, e_row,
    a_s, a_r, g_s, g_r, u_r, f_s, d_s, d_r, x_s, x_r, t_s, t_r, v_s, v_r, e1_s, e1_r, e2_s, e2_r, i_s, o_s,
):
    row = lax.axis_index("row")
    col = lax.axis_index("col")
    x_lo, y = row // 4, row % 4
    z, x_hi, core = col // 4, (col // 2) % 2, col % 2
    colchip = col // 2

    def at_y(d):
        return {"row": x_lo * 4 + (y + d) % 4}

    def at_z(d):
        return {"col": ((z + d) % 4) * 4 + x_hi * 2 + core}

    def at_x(d):
        xx = (x_hi * 2 + x_lo + d) % 4
        return {"row": (xx % 2) * 4 + y, "col": (z * 2 + xx // 2) * 2 + core}

    sibling = {"col": colchip * 2 + 1 - core}

    def partner(h):
        return {"row": colchip, "col": row * 2 + h}

    inputs = [
        pltpu.make_async_copy(src, dst, i_s.at[n])
        for n, (src, dst) in enumerate([(slab_hbm, slab), (occ_hbm, occ), (vir_hbm, vir)])
    ]
    for cp in inputs:
        cp.start()
    bar = pltpu.get_barrier_semaphore()
    for d in range(1, 8):
        pl.semaphore_signal(bar, inc=1, device_id={"row": (row + d) % 8})
    for d in range(1, 16):
        pl.semaphore_signal(bar, inc=1, device_id={"col": (col + d) % 16})
    pl.semaphore_signal(
        bar, inc=1, device_id={"row": (1 - x_lo) * 4 + y, "col": (z * 2 + 1 - x_hi) * 2 + core}
    )

    @pl.when(row != colchip)
    def _():
        for h in range(2):
            pl.semaphore_signal(bar, inc=1, device_id=partner(h))

    me_x = x_hi * 2 + x_lo
    relay_row = x_lo * 4 + colchip % 4
    relay_chip = (row // 2) * 2 + x_hi
    to_x = (row % 2) * 2 + colchip // 4
    hop_x = (to_x - me_x + 4) % 4
    by_relay = (hop_x != 0) & ((relay_row != row) | (relay_chip != colchip))

    def source(k):
        xx = (me_x + k) % 4
        y_s = (z % 2) * 2 + xx // 2
        z_s = (xx % 2) * 2 + y // 2
        there = (x_hi == y % 2) & (x_lo == z // 2) & ((y_s != y) | (z_s != z))
        return x_lo * 4 + y_s, z_s * 2 + x_hi, there

    for k in range(1, 4):
        row_s, chip_s, there = source(k)

        @pl.when(there)
        def _():
            for h in range(2):
                pl.semaphore_signal(bar, inc=1, device_id={"row": row_s, "col": chip_s * 2 + h})

    def stage(o):
        v = slab[:, o, :]
        for k in range(4):
            send_l[o, k, :, 0:256] = v[:, k * 256 : k * 256 + 256]
            send_l[o, k, :, 256:512] = v[:, 1024 + k * 256 : 1280 + k * 256]
        w = slab[:, 3 - o, :]
        for k in range(4):
            for c in range(2):
                for h in range(2):
                    b = k * 512 + h * 256 + c * 128
                    send_r[o, k, :, c * 256 + h * 128 : c * 256 + h * 128 + 128] = w[:, b : b + 128]
        left[o, z, y] = send_l[o, y]
        right[o, y, z] = send_r[o, z]

    for cp in inputs:
        cp.wait()
    stage(0)
    pl.semaphore_wait(bar, 23 + jnp.where(row == colchip, 0, 2) + jnp.where(by_relay, 2, 0))

    def copy(src, dst, ssem, rsem, to):
        cp = pltpu.make_async_remote_copy(src, dst, ssem, rsem, device_id=to)
        cp.start()
        return cp

    def took(sem, like):
        pltpu.make_async_copy(like, like, sem).wait()

    scatter, gather = {}, {}

    def post_scatter(o):
        for d in (1, 3, 2):
            ky, kz = (y + d) % 4, (z + d) % 4
            scatter[o, 0, d] = copy(
                send_l.at[o, ky], left.at[o, z, y], a_s, a_r.at[0, o, d - 1], at_y(d)
            )
            scatter[o, 1, d] = copy(
                send_r.at[o, kz], right.at[o, y, z], a_s, a_r.at[1, o, d - 1], at_z(d)
            )

    def post_gather(o, d):
        ky, kz = (y - d) % 4, (z - d) % 4
        for way, step in ((0, 1), (1, 3)):
            sems = [g_r.at[side, o, d] if way == d % 2 else u_r.at[side, o] for side in range(2)]
            gather[o, 0, way, d] = copy(left.at[o, z, ky], left.at[o, z, ky], g_s, sems[0], at_z(step))
            gather[o, 1, way, d] = copy(right.at[o, y, kz], right.at[o, y, kz], g_s, sems[1], at_y(step))

    def rest_gather(o):
        for d in (1, 3, 2):
            scatter[o, 0, d].wait_recv()
            scatter[o, 1, d].wait_recv()
            post_gather(o, d)

    def forward(o, d):
        way, step = (0, 1) if d % 2 == 0 else (1, 3)
        kz, ky = (z - step) % 4, (y - step) % 4
        jy, jz = (y - d) % 4, (z - d) % 4
        gather[o, 0, way, d].wait_recv()
        copy(left.at[o, kz, jy], left.at[o, kz, jy], f_s, u_r.at[0, o], at_z(step))
        gather[o, 1, way, d].wait_recv()
        copy(right.at[o, ky, jz], right.at[o, ky, jz], f_s, u_r.at[1, o], at_y(step))

    def prepare(o):
        took(u_r.at[0, o], left.at[o, 0:2])
        took(u_r.at[1, o], right.at[o, 0:2])
        for k in range(4):
            v = left[o, k].reshape(128, 512).T
            hi = v.astype(BF16)
            lt_hi[o, :, k * 128 : k * 128 + 128] = hi
            lt_lo[o, :, k * 128 : k * 128 + 128] = (v - hi.astype(F32)).astype(BF16)
        for kz in range(4):
            for ky in range(4):
                w = right[o, ky, kz]
                hi = w.astype(BF16)
                lo = (w - hi.astype(F32)).astype(BF16)
                q = kz * 128 + ky * 32
                for h in range(2):
                    r_hi[o, h, q : q + 32, :] = hi[:, h * 256 : h * 256 + 256]
                    r_lo[o, h, q : q + 32, :] = lo[:, h * 256 : h * 256 + 256]

    def multiply(s, which, half):
        lo_, ro_, _ = SEQ[s]

        @pl.loop(0, 2)
        def _(ab):
            rows = pl.ds(pl.multiple_of(ab * 256, 256), 256)
            hi = lt_hi[lo_, rows, :]
            acc = jnp.dot(hi, r_hi[ro_, half], preferred_element_type=F32)
            acc += jnp.dot(hi, r_lo[ro_, half], preferred_element_type=F32)
            acc += jnp.dot(lt_lo[lo_, rows, :], r_hi[ro_, half], preferred_element_type=F32)
            part[s, which, ab] = acc[:, 0:128]
            part[s, which, 2 + ab] = acc[:, 128:256]

    exchanged, along_x = {}, {}

    def compute(s):
        multiply(s, 0, 1 - core)
        exchanged[s] = copy(part.at[s, 0], part_in.at[s], d_s, d_r.at[s], sibling)
        multiply(s, 1, core)

    up_x, down_x, far_x = (me_x + 1) % 4, (me_x + 3) % 4, (me_x + 2) % 4
    low, high = pl.ds(0, 128), pl.ds(128, 128)

    def reduce(s):
        exchanged[s].wait_recv()
        part[s, 1] = part[s, 1] + part_in[s]
        mine = part.at[s, 1]
        along_x[s, 0] = copy(mine.at[far_x, low], x_via.at[s, 0], x_s, x_r.at[s, 0], at_x(1))
        along_x[s, 1] = copy(mine.at[far_x, high], x_via.at[s, 1], x_s, x_r.at[s, 1], at_x(3))
        copy(mine.at[up_x, high], x_in.at[s, 0, high], x_s, x_r.at[s, 2], at_x(1))
        copy(mine.at[down_x, low], x_in.at[s, 1, low], x_s, x_r.at[s, 2], at_x(3))

    def reduce_on(s):
        mine = part.at[s, 1]
        along_x[s, 0].wait_recv()
        part[s, 1, up_x, 0:128] = part[s, 1, up_x, 0:128] + x_via[s, 0]
        copy(mine.at[up_x, low], x_in.at[s, 0, low], x_s, x_r.at[s, 2], at_x(1))
        along_x[s, 1].wait_recv()
        part[s, 1, down_x, 128:256] = part[s, 1, down_x, 128:256] + x_via[s, 1]
        copy(mine.at[down_x, high], x_in.at[s, 1, high], x_s, x_r.at[s, 2], at_x(3))

    def swap(s, h, part_no):
        rows = pl.ds(pl.multiple_of(h * 128 + part_no * 64, 64), 64)
        return pltpu.make_async_remote_copy(
            dfin.at[s, rows], t_in.at[s, core, pl.ds(part_no * 64, 64)],
            t_s.at[s], t_r.at[s], device_id=partner(h),
        )

    def swap_by_relay(s, h):
        rows = pl.ds(pl.multiple_of(h * 128 + 64, 64), 64)
        return pltpu.make_async_remote_copy(
            dfin.at[s, rows], via.at[s, hop_x - 1, core], t_s.at[s], v_r.at[s, hop_x - 1],
            device_id={"row": relay_row, "col": relay_chip * 2 + h},
        )

    def onto(s, k, c):
        row_s, chip_s, _ = source(k)
        return pltpu.make_async_remote_copy(
            via.at[s, k - 1, c], t_in.at[s, c, pl.ds(64, 64)], v_s.at[s, k - 1], t_r.at[s],
            device_id={"row": chip_s, "col": row_s * 2 + core},
        )

    def relays(s, k):
        row_s, chip_s, there = source(k)
        return there & (row_s < chip_s if s % 2 == 0 else row_s > chip_s)

    def relay(s):
        for k in range(1, 4):

            @pl.when(relays(s, k))
            def _():
                took(v_r.at[s, k - 1], via.at[s, k - 1])
                for c in range(2):
                    onto(s, k, c).start()

    def swap_sibling(s):
        return pltpu.make_async_remote_copy(
            dfin.at[s, pl.ds(pl.multiple_of((1 - core) * 128, 128), 128)], t_in.at[s, core],
            t_s.at[s], t_r.at[s], device_id=sibling,
        )

    def sends(s):
        return row < colchip if s % 2 == 0 else row > colchip

    def receives(s):
        return row > colchip if s % 2 == 0 else row < colchip

    written = []
    vir_b = vir[pl.ds(col, 1), :]

    def finish(s):
        took(x_r.at[s, 2], x_in.at[s])
        p = SEQ[s][2]
        i, j = PAIRS[p]
        total = part[s, 1, me_x] + (x_in[s, 0] + x_in[s, 1])
        dfin[s] = total

        amp = total / (((occ[i] + occ[j]) - vir_a[...]) - vir_b)
        amps[p] = amp
        written.append(pltpu.make_async_copy(amps.at[p], amps_hbm.at[p], o_s.at[p]))
        written[-1].start()
        e_acc[p] = jnp.sum((2.0 * (amp * total)).reshape(32, 8, 128), axis=0)

    def swap_start(s):
        @pl.when(sends(s))
        def _():
            for h in range(2):
                swap(s, h, 0).start()

        @pl.when(sends(s) & by_relay)
        def _():
            for h in range(2):
                swap_by_relay(s, h).start()

        @pl.when(sends(s) & jnp.logical_not(by_relay))
        def _():
            for h in range(2):
                swap(s, h, 1).start()

        @pl.when(row == colchip)
        def _():
            swap_sibling(s).start()
            t_in[s, core] = dfin[s, pl.ds(pl.multiple_of(core * 128, 128), 128), :]

    def swap_sent(s):
        @pl.when(sends(s))
        def _():
            took(t_s.at[s], dfin.at[s])

        @pl.when(row == colchip)
        def _():
            took(t_s.at[s], t_in.at[s, 0])

        for k in range(1, 4):

            @pl.when(relays(s, k))
            def _():
                took(v_s.at[s, k - 1], via.at[s, k - 1])

    def energy_swapped(s, weight):
        p = SEQ[s][2]
        prod = amps[p, 0:128] * t_in[s, 0].T + amps[p, 128:256] * t_in[s, 1].T
        e_acc[p] = e_acc[p] - weight * jnp.sum(prod.reshape(16, 8, 128), axis=0)

    def swapped(s):
        @pl.when(receives(s))
        def _():
            took(t_r.at[s], t_in.at[s])
            energy_swapped(s, 2.0)

        @pl.when(row == colchip)
        def _():
            took(t_r.at[s], t_in.at[s, 1 - core])
            energy_swapped(s, 1.0)

    def forward_rest(o):
        for d in (1, 3, 2):
            forward(o, d)

    post_scatter(0)
    post_gather(0, 0)
    stage(1)
    rest_gather(0)
    forward(0, 0)
    post_scatter(1)
    post_gather(1, 0)
    stage(2)
    for h in range(2):
        vir_a[h * 128 : h * 128 + 128, :] = jnp.broadcast_to(vir[pl.ds(row * 2 + h, 1), :], (128, 128)).T
    forward_rest(0)
    rest_gather(1)
    forward(1, 0)
    post_scatter(2)
    post_gather(2, 0)
    prepare(0)
    compute(0)
    reduce(0)
    forward_rest(1)
    reduce_on(0)
    rest_gather(2)
    forward(2, 0)
    finish(0)
    prepare(1)
    compute(1)
    compute(2)
    reduce(1)
    compute(3)
    reduce(2)
    reduce(3)
    forward_rest(2)
    swap_start(0)
    reduce_on(1)
    prepare(2)
    compute(4)
    reduce_on(2)
    compute(5)
    reduce(4)
    reduce_on(3)
    reduce(5)
    relay(0)
    finish(1)
    swap_start(1)
    finish(2)
    reduce_on(4)
    swap_start(2)
    relay(1)
    reduce_on(5)
    finish(3)
    swap_start(3)
    relay(2)
    relay(3)
    finish(4)
    swap_start(4)
    finish(5)
    swap_start(5)
    for s in range(4):
        swapped(s)
    relay(4)
    relay(5)
    swapped(4)
    swapped(5)

    e_tile = jnp.concatenate(
        [jnp.sum(e_acc[p], axis=0, keepdims=True) for p in range(6)] + [jnp.zeros((2, 128), F32)], axis=0
    )
    e_col[col] = e_tile
    for d in range(1, 16):
        copy(e_col.at[col], e_col.at[col], e1_s, e1_r, {"col": (col + d) % 16})
    took(a_s, left.at[:, 0:3, 0:2])
    took(g_s, left)
    took(f_s, left.at[:, 0:2])
    took(d_s, part_in)
    took(x_s, part.at[:, 0, 0:3])
    for s in range(6):
        swap_sent(s)
    took(e1_r, e_col.at[0:15])
    e_row[row] = jnp.sum(e_col[...], axis=0)
    for d in range(1, 8):
        copy(e_row.at[row], e_row.at[row], e2_s, e2_r, {"row": (row + d) % 8})
    took(e1_s, e_col.at[0:15])
    took(e2_r, e_row.at[0:7])
    whole = jnp.sum(jnp.sum(e_row[...], axis=0), axis=1, keepdims=True)
    energy[...] = jnp.broadcast_to(whole * (2.0 / (NV * NV)), (8, 128))
    took(e2_s, e_row.at[0:7])
    for cp in written:
        cp.wait()


def local(slab, occ_energy, vir_energy):
    dma = pltpu.SemaphoreType.DMA
    vmem = pltpu.VMEM
    amps, energy = pl.pallas_call(
        kernel,
        out_shape=(
            jax.ShapeDtypeStruct((6, 256, 128), F32),
            jax.ShapeDtypeStruct((8, 128), F32),
        ),
        in_specs=[pl.BlockSpec(memory_space=pltpu.HBM)] * 3,
        out_specs=(pl.BlockSpec(memory_space=pltpu.HBM), pl.BlockSpec(memory_space=vmem)),
        scratch_shapes=[
            vmem((NQ, 4, NV), F32),
            pltpu.SMEM((4,), F32),
            vmem((16, 128), F32),
            vmem((6, 256, 128), F32),
            vmem((3, 4, NQ, 512), F32),
            vmem((3, 4, NQ, 512), F32),
            vmem((3, 4, 4, NQ, 512), F32),
            vmem((3, 4, 4, NQ, 512), F32),
            vmem((3, 512, 512), BF16),
            vmem((3, 512, 512), BF16),
            vmem((3, 2, 512, 256), BF16),
            vmem((3, 2, 512, 256), BF16),
            vmem((6, 2, 4, 256, 128), F32),
            vmem((6, 4, 256, 128), F32),
            vmem((6, 2, 256, 128), F32),
            vmem((6, 2, 128, 128), F32),
            vmem((6, 256, 128), F32),
            vmem((6, 2, 128, 128), F32),
            vmem((6, 3, 2, 64, 128), F32),
            vmem((256, 128), F32),
            vmem((6, 8, 128), F32),
            vmem((16, 8, 128), F32),
            vmem((8, 8, 128), F32),
            dma,
            dma((2, 3, 3)),
            dma,
            dma((2, 3, 4)),
            dma((2, 3)),
            dma,
            dma,
            dma((6,)),
            dma,
            dma((6, 3)),
            dma((6,)),
            dma((6,)),
            dma((6, 3)),
            dma((6, 3)),
            dma,
            dma,
            dma,
            dma,
            dma((3,)),
            dma((6,)),
        ],
        compiler_params=pltpu.CompilerParams(
            collective_id=0, has_side_effects=True, vmem_limit_bytes=60 * 2**20
        ),
        name="pairs",
    )(slab, occ_energy, vir_energy.reshape(16, 128))
    return amps, energy[:6, 0]


def solution(mesh):
    return jax.shard_map(
        local,
        mesh=mesh,
        in_specs=(P(("row", "col"), None, None), P(), P()),
        out_specs=(P(None, "row", "col"), P()),
        check_vma=False,
    )
```

```python
import jax
import jax.numpy as jnp
from jax import lax
from jax.experimental import pallas as pl
from jax.experimental.pallas import tpu as pltpu
from jax.sharding import PartitionSpec as P

F32, BF16 = jnp.float32, jnp.bfloat16
NQ = 32
NV = 2048
SEQ = [(0, 0, 2), (0, 1, 1), (1, 0, 4), (1, 1, 3), (0, 2, 0), (2, 0, 5)]
PAIRS = [(0, 1), (0, 2), (0, 3), (1, 2), (1, 3), (2, 3)]


def kernel(
    slab_hbm, occ_hbm, vir_hbm, amps_hbm, energy,
    slab, occ, vir, amps,
    send_l, send_r, left, right, lt_hi, lt_lo, r_hi, r_lo,
    part, part_in, x_in, x_via, dfin, t_in, via, vir_a, e_acc, e_col, e_row,
    a_s, a_r, g_s, g_r, u_r, f_s, d_s, d_r, x_s, x_r, t_s, t_r, v_s, v_r, e1_s, e1_r, e2_s, e2_r, i_s, o_s,
):
    row = lax.axis_index("row")
    col = lax.axis_index("col")
    x_lo, y = row // 4, row % 4
    z, x_hi, core = col // 4, (col // 2) % 2, col % 2
    colchip = col // 2

    def at_y(d):
        return {"row": x_lo * 4 + (y + d) % 4}

    def at_z(d):
        return {"col": ((z + d) % 4) * 4 + x_hi * 2 + core}

    def at_x(d):
        xx = (x_hi * 2 + x_lo + d) % 4
        return {"row": (xx % 2) * 4 + y, "col": (z * 2 + xx // 2) * 2 + core}

    sibling = {"col": colchip * 2 + 1 - core}

    def partner(h):
        return {"row": colchip, "col": row * 2 + h}

    inputs = [
        pltpu.make_async_copy(src, dst, i_s.at[n])
        for n, (src, dst) in enumerate([(slab_hbm, slab), (occ_hbm, occ), (vir_hbm, vir)])
    ]
    for cp in inputs:
        cp.start()
    bar = pltpu.get_barrier_semaphore()
    for d in range(1, 8):
        pl.semaphore_signal(bar, inc=1, device_id={"row": (row + d) % 8})
    for d in range(1, 16):
        pl.semaphore_signal(bar, inc=1, device_id={"col": (col + d) % 16})
    pl.semaphore_signal(
        bar, inc=1, device_id={"row": (1 - x_lo) * 4 + y, "col": (z * 2 + 1 - x_hi) * 2 + core}
    )

    @pl.when(row != colchip)
    def _():
        for h in range(2):
            pl.semaphore_signal(bar, inc=1, device_id=partner(h))

    me_x = x_hi * 2 + x_lo
    relay_row = x_lo * 4 + colchip % 4
    relay_chip = (row // 2) * 2 + x_hi
    to_x = (row % 2) * 2 + colchip // 4
    hop_x = (to_x - me_x + 4) % 4
    by_relay = (hop_x != 0) & ((relay_row != row) | (relay_chip != colchip))

    def source(k):
        xx = (me_x + k) % 4
        y_s = (z % 2) * 2 + xx // 2
        z_s = (xx % 2) * 2 + y // 2
        there = (x_hi == y % 2) & (x_lo == z // 2) & ((y_s != y) | (z_s != z))
        return x_lo * 4 + y_s, z_s * 2 + x_hi, there

    for k in range(1, 4):
        row_s, chip_s, there = source(k)

        @pl.when(there)
        def _():
            for h in range(2):
                pl.semaphore_signal(bar, inc=1, device_id={"row": row_s, "col": chip_s * 2 + h})

    def stage(o):
        v = slab[:, o, :]
        for k in range(4):
            send_l[o, k, :, 0:256] = v[:, k * 256 : k * 256 + 256]
            send_l[o, k, :, 256:512] = v[:, 1024 + k * 256 : 1280 + k * 256]
        w = slab[:, 3 - o, :]
        for k in range(4):
            for c in range(2):
                for h in range(2):
                    b = k * 512 + h * 256 + c * 128
                    send_r[o, k, :, c * 256 + h * 128 : c * 256 + h * 128 + 128] = w[:, b : b + 128]
        left[o, z, y] = send_l[o, y]
        right[o, y, z] = send_r[o, z]

    for cp in inputs:
        cp.wait()
    stage(0)
    pl.semaphore_wait(bar, 23 + jnp.where(row == colchip, 0, 2) + jnp.where(by_relay, 2, 0))

    def copy(src, dst, ssem, rsem, to):
        cp = pltpu.make_async_remote_copy(src, dst, ssem, rsem, device_id=to)
        cp.start()
        return cp

    def took(sem, like):
        pltpu.make_async_copy(like, like, sem).wait()

    scatter, gather = {}, {}

    def post_scatter(o):
        for d in (1, 3, 2):
            ky, kz = (y + d) % 4, (z + d) % 4
            scatter[o, 0, d] = copy(
                send_l.at[o, ky], left.at[o, z, y], a_s, a_r.at[0, o, d - 1], at_y(d)
            )
            scatter[o, 1, d] = copy(
                send_r.at[o, kz], right.at[o, y, z], a_s, a_r.at[1, o, d - 1], at_z(d)
            )

    def post_gather(o, d):
        ky, kz = (y - d) % 4, (z - d) % 4
        for way, step in ((0, 1), (1, 3)):
            sems = [g_r.at[side, o, d] if way == d % 2 else u_r.at[side, o] for side in range(2)]
            gather[o, 0, way, d] = copy(left.at[o, z, ky], left.at[o, z, ky], g_s, sems[0], at_z(step))
            gather[o, 1, way, d] = copy(right.at[o, y, kz], right.at[o, y, kz], g_s, sems[1], at_y(step))

    def rest_gather(o):
        for d in (1, 3, 2):
            scatter[o, 0, d].wait_recv()
            scatter[o, 1, d].wait_recv()
            post_gather(o, d)

    def forward(o, d):
        way, step = (0, 1) if d % 2 == 0 else (1, 3)
        kz, ky = (z - step) % 4, (y - step) % 4
        jy, jz = (y - d) % 4, (z - d) % 4
        gather[o, 0, way, d].wait_recv()
        copy(left.at[o, kz, jy], left.at[o, kz, jy], f_s, u_r.at[0, o], at_z(step))
        gather[o, 1, way, d].wait_recv()
        copy(right.at[o, ky, jz], right.at[o, ky, jz], f_s, u_r.at[1, o], at_y(step))

    def prepare(o):
        took(u_r.at[0, o], left.at[o, 0:2])
        took(u_r.at[1, o], right.at[o, 0:2])
        for k in range(4):
            v = left[o, k].reshape(128, 512).T
            hi = v.astype(BF16)
            lt_hi[o, :, k * 128 : k * 128 + 128] = hi
            lt_lo[o, :, k * 128 : k * 128 + 128] = (v - hi.astype(F32)).astype(BF16)
        for kz in range(4):
            for ky in range(4):
                w = right[o, ky, kz]
                hi = w.astype(BF16)
                lo = (w - hi.astype(F32)).astype(BF16)
                q = kz * 128 + ky * 32
                for h in range(2):
                    r_hi[o, h, q : q + 32, :] = hi[:, h * 256 : h * 256 + 256]
                    r_lo[o, h, q : q + 32, :] = lo[:, h * 256 : h * 256 + 256]

    def multiply(s, which, half):
        lo_, ro_, _ = SEQ[s]

        @pl.loop(0, 2)
        def _(ab):
            rows = pl.ds(pl.multiple_of(ab * 256, 256), 256)
            hi = lt_hi[lo_, rows, :]
            acc = jnp.dot(hi, r_hi[ro_, half], preferred_element_type=F32)
            acc += jnp.dot(hi, r_lo[ro_, half], preferred_element_type=F32)
            acc += jnp.dot(lt_lo[lo_, rows, :], r_hi[ro_, half], preferred_element_type=F32)
            part[s, which, ab] = acc[:, 0:128]
            part[s, which, 2 + ab] = acc[:, 128:256]

    exchanged, along_x = {}, {}

    def compute(s):
        multiply(s, 0, 1 - core)
        exchanged[s] = copy(part.at[s, 0], part_in.at[s], d_s, d_r.at[s], sibling)
        multiply(s, 1, core)

    up_x, down_x, far_x = (me_x + 1) % 4, (me_x + 3) % 4, (me_x + 2) % 4
    low, high = pl.ds(0, 128), pl.ds(128, 128)

    def reduce(s):
        exchanged[s].wait_recv()
        part[s, 1] = part[s, 1] + part_in[s]
        mine = part.at[s, 1]
        along_x[s, 0] = copy(mine.at[far_x, low], x_via.at[s, 0], x_s, x_r.at[s, 0], at_x(1))
        along_x[s, 1] = copy(mine.at[far_x, high], x_via.at[s, 1], x_s, x_r.at[s, 1], at_x(3))
        copy(mine.at[up_x, high], x_in.at[s, 0, high], x_s, x_r.at[s, 2], at_x(1))
        copy(mine.at[down_x, low], x_in.at[s, 1, low], x_s, x_r.at[s, 2], at_x(3))

    def reduce_on(s):
        mine = part.at[s, 1]
        along_x[s, 0].wait_recv()
        part[s, 1, up_x, 0:128] = part[s, 1, up_x, 0:128] + x_via[s, 0]
        copy(mine.at[up_x, low], x_in.at[s, 0, low], x_s, x_r.at[s, 2], at_x(1))
        along_x[s, 1].wait_recv()
        part[s, 1, down_x, 128:256] = part[s, 1, down_x, 128:256] + x_via[s, 1]
        copy(mine.at[down_x, high], x_in.at[s, 1, high], x_s, x_r.at[s, 2], at_x(3))

    def swap(s, h, part_no):
        rows = pl.ds(pl.multiple_of(h * 128 + part_no * 64, 64), 64)
        return pltpu.make_async_remote_copy(
            dfin.at[s, rows], t_in.at[s, core, pl.ds(part_no * 64, 64)],
            t_s.at[s], t_r.at[s], device_id=partner(h),
        )

    def swap_by_relay(s, h):
        rows = pl.ds(pl.multiple_of(h * 128 + 64, 64), 64)
        return pltpu.make_async_remote_copy(
            dfin.at[s, rows], via.at[s, hop_x - 1, core], t_s.at[s], v_r.at[s, hop_x - 1],
            device_id={"row": relay_row, "col": relay_chip * 2 + h},
        )

    def onto(s, k, c):
        row_s, chip_s, _ = source(k)
        return pltpu.make_async_remote_copy(
            via.at[s, k - 1, c], t_in.at[s, c, pl.ds(64, 64)], v_s.at[s, k - 1], t_r.at[s],
            device_id={"row": chip_s, "col": row_s * 2 + core},
        )

    def relays(s, k):
        row_s, chip_s, there = source(k)
        return there & (row_s < chip_s if s % 2 == 0 else row_s > chip_s)

    def relay(s):
        for k in range(1, 4):

            @pl.when(relays(s, k))
            def _():
                took(v_r.at[s, k - 1], via.at[s, k - 1])
                for c in range(2):
                    onto(s, k, c).start()

    def swap_sibling(s):
        return pltpu.make_async_remote_copy(
            dfin.at[s, pl.ds(pl.multiple_of((1 - core) * 128, 128), 128)], t_in.at[s, core],
            t_s.at[s], t_r.at[s], device_id=sibling,
        )

    def sends(s):
        return row < colchip if s % 2 == 0 else row > colchip

    def receives(s):
        return row > colchip if s % 2 == 0 else row < colchip

    written = []
    vir_b = vir[pl.ds(col, 1), :]

    def finish(s):
        took(x_r.at[s, 2], x_in.at[s])
        p = SEQ[s][2]
        i, j = PAIRS[p]
        total = part[s, 1, me_x] + (x_in[s, 0] + x_in[s, 1])
        dfin[s] = total

        amp = total / (((occ[i] + occ[j]) - vir_a[...]) - vir_b)
        amps[p] = amp
        written.append(pltpu.make_async_copy(amps.at[p], amps_hbm.at[p], o_s.at[p]))
        written[-1].start()
        e_acc[p] = jnp.sum((2.0 * (amp * total)).reshape(32, 8, 128), axis=0)

    def swap_start(s):
        @pl.when(sends(s))
        def _():
            for h in range(2):
                swap(s, h, 0).start()

        @pl.when(sends(s) & by_relay)
        def _():
            for h in range(2):
                swap_by_relay(s, h).start()

        @pl.when(sends(s) & jnp.logical_not(by_relay))
        def _():
            for h in range(2):
                swap(s, h, 1).start()

        @pl.when(row == colchip)
        def _():
            swap_sibling(s).start()
            t_in[s, core] = dfin[s, pl.ds(pl.multiple_of(core * 128, 128), 128), :]

    def swap_sent(s):
        @pl.when(sends(s))
        def _():
            took(t_s.at[s], dfin.at[s])

        @pl.when(row == colchip)
        def _():
            took(t_s.at[s], t_in.at[s, 0])

        for k in range(1, 4):

            @pl.when(relays(s, k))
            def _():
                took(v_s.at[s, k - 1], via.at[s, k - 1])

    def energy_swapped(s, weight):
        p = SEQ[s][2]
        prod = amps[p, 0:128] * t_in[s, 0].T + amps[p, 128:256] * t_in[s, 1].T
        e_acc[p] = e_acc[p] - weight * jnp.sum(prod.reshape(16, 8, 128), axis=0)

    def swapped(s):
        @pl.when(receives(s))
        def _():
            took(t_r.at[s], t_in.at[s])
            energy_swapped(s, 2.0)

        @pl.when(row == colchip)
        def _():
            took(t_r.at[s], t_in.at[s, 1 - core])
            energy_swapped(s, 1.0)

    def forward_rest(o):
        for d in (1, 3, 2):
            forward(o, d)

    post_scatter(0)
    post_gather(0, 0)
    stage(1)
    rest_gather(0)
    forward(0, 0)
    post_scatter(1)
    post_gather(1, 0)
    stage(2)
    for h in range(2):
        vir_a[h * 128 : h * 128 + 128, :] = jnp.broadcast_to(vir[pl.ds(row * 2 + h, 1), :], (128, 128)).T
    forward_rest(0)
    rest_gather(1)
    forward(1, 0)
    post_scatter(2)
    post_gather(2, 0)
    prepare(0)
    compute(0)
    reduce(0)
    forward_rest(1)
    reduce_on(0)
    rest_gather(2)
    forward(2, 0)
    finish(0)
    prepare(1)
    compute(1)
    compute(2)
    reduce(1)
    compute(3)
    reduce(2)
    reduce(3)
    forward_rest(2)
    swap_start(0)
    reduce_on(1)
    prepare(2)
    compute(4)
    reduce_on(2)
    compute(5)
    reduce(4)
    reduce_on(3)
    reduce(5)
    relay(0)
    finish(1)
    swap_start(1)
    finish(2)
    reduce_on(4)
    swap_start(2)
    relay(1)
    reduce_on(5)
    finish(3)
    swap_start(3)
    relay(2)
    relay(3)
    finish(4)
    swap_start(4)
    finish(5)
    swap_start(5)
    for s in range(4):
        swapped(s)
    relay(4)
    relay(5)
    swapped(4)
    swapped(5)

    e_tile = jnp.concatenate(
        [jnp.sum(e_acc[p], axis=0, keepdims=True) for p in range(6)] + [jnp.zeros((2, 128), F32)], axis=0
    )
    e_col[col] = e_tile
    for d in range(1, 16):
        copy(e_col.at[col], e_col.at[col], e1_s, e1_r, {"col": (col + d) % 16})
    took(a_s, left.at[:, 0:3, 0:2])
    took(g_s, left)
    took(f_s, left.at[:, 0:2])
    took(d_s, part_in)
    took(x_s, part.at[:, 0, 0:3])
    for s in range(6):
        swap_sent(s)
    took(e1_r, e_col.at[0:15])
    e_row[row] = jnp.sum(e_col[...], axis=0)
    for d in range(1, 8):
        copy(e_row.at[row], e_row.at[row], e2_s, e2_r, {"row": (row + d) % 8})
    took(e1_s, e_col.at[0:15])
    took(e2_r, e_row.at[0:7])
    whole = jnp.sum(e_row[...], axis=0)
    for p in range(6):
        energy[p] = jnp.sum(whole[p : p + 1]) * (2.0 / (NV * NV))
    took(e2_s, e_row.at[0:7])
    for cp in written:
        cp.wait()


def local(slab, occ_energy, vir_energy):
    dma = pltpu.SemaphoreType.DMA
    vmem = pltpu.VMEM
    amps, energy = pl.pallas_call(
        kernel,
        out_shape=(
            jax.ShapeDtypeStruct((6, 256, 128), F32),
            jax.ShapeDtypeStruct((6,), F32),
        ),
        in_specs=[pl.BlockSpec(memory_space=pltpu.HBM)] * 3,
        out_specs=(pl.BlockSpec(memory_space=pltpu.HBM), pl.BlockSpec(memory_space=pltpu.SMEM)),
        scratch_shapes=[
            vmem((NQ, 4, NV), F32),
            pltpu.SMEM((4,), F32),
            vmem((16, 128), F32),
            vmem((6, 256, 128), F32),
            vmem((3, 4, NQ, 512), F32),
            vmem((3, 4, NQ, 512), F32),
            vmem((3, 4, 4, NQ, 512), F32),
            vmem((3, 4, 4, NQ, 512), F32),
            vmem((3, 512, 512), BF16),
            vmem((3, 512, 512), BF16),
            vmem((3, 2, 512, 256), BF16),
            vmem((3, 2, 512, 256), BF16),
            vmem((6, 2, 4, 256, 128), F32),
            vmem((6, 4, 256, 128), F32),
            vmem((6, 2, 256, 128), F32),
            vmem((6, 2, 128, 128), F32),
            vmem((6, 256, 128), F32),
            vmem((6, 2, 128, 128), F32),
            vmem((6, 3, 2, 64, 128), F32),
            vmem((256, 128), F32),
            vmem((6, 8, 128), F32),
            vmem((16, 8, 128), F32),
            vmem((8, 8, 128), F32),
            dma,
            dma((2, 3, 3)),
            dma,
            dma((2, 3, 4)),
            dma((2, 3)),
            dma,
            dma,
            dma((6,)),
            dma,
            dma((6, 3)),
            dma((6,)),
            dma((6,)),
            dma((6, 3)),
            dma((6, 3)),
            dma,
            dma,
            dma,
            dma,
            dma((3,)),
            dma((6,)),
        ],
        compiler_params=pltpu.CompilerParams(
            collective_id=0, has_side_effects=True, vmem_limit_bytes=60 * 2**20
        ),
        name="pairs",
    )(slab, occ_energy, vir_energy.reshape(16, 128))
    return amps, energy


def solution(mesh):
    return jax.shard_map(
        local,
        mesh=mesh,
        in_specs=(P(("row", "col"), None, None), P(), P()),
        out_specs=(P(None, "row", "col"), P()),
        check_vma=False,
    )
```

```python
import jax
import jax.numpy as jnp
from jax import lax
from jax.experimental import pallas as pl
from jax.experimental.pallas import tpu as pltpu
from jax.sharding import PartitionSpec as P

F32, BF16 = jnp.float32, jnp.bfloat16
NQ = 32
NV = 2048
SEQ = [(0, 0, 2), (0, 1, 1), (1, 0, 4), (1, 1, 3), (0, 2, 0), (2, 0, 5)]
PAIRS = [(0, 1), (0, 2), (0, 3), (1, 2), (1, 3), (2, 3)]


def kernel(
    slab_hbm, occ_hbm, vir_hbm, amps_hbm, energy,
    slab, occ, vir, amps,
    send_l, send_r, left, right, lt_hi, lt_lo, r_hi, r_lo,
    part, part_in, x_in, x_via, dfin, t_in, via, vir_a, e_acc, e_col, e_row,
    a_s, a_r, g_s, g_r, u_r, f_s, d_s, d_r, x_s, x_r, t_s, t_r, v_s, v_r, e1_s, e1_r, e2_s, e2_r, i_s, o_s,
):
    row = lax.axis_index("row")
    col = lax.axis_index("col")
    x_lo, y = row // 4, row % 4
    z, x_hi, core = col // 4, (col // 2) % 2, col % 2
    colchip = col // 2

    def at_y(d):
        return {"row": x_lo * 4 + (y + d) % 4}

    def at_z(d):
        return {"col": ((z + d) % 4) * 4 + x_hi * 2 + core}

    def at_x(d):
        xx = (x_hi * 2 + x_lo + d) % 4
        return {"row": (xx % 2) * 4 + y, "col": (z * 2 + xx // 2) * 2 + core}

    sibling = {"col": colchip * 2 + 1 - core}

    def partner(h):
        return {"row": colchip, "col": row * 2 + h}

    inputs = [
        pltpu.make_async_copy(src, dst, i_s.at[n])
        for n, (src, dst) in enumerate([(slab_hbm, slab), (occ_hbm, occ), (vir_hbm, vir)])
    ]
    for cp in inputs:
        cp.start()
    bar = pltpu.get_barrier_semaphore()
    for d in range(1, 8):
        pl.semaphore_signal(bar, inc=1, device_id={"row": (row + d) % 8})
    for d in range(1, 16):
        pl.semaphore_signal(bar, inc=1, device_id={"col": (col + d) % 16})
    pl.semaphore_signal(
        bar, inc=1, device_id={"row": (1 - x_lo) * 4 + y, "col": (z * 2 + 1 - x_hi) * 2 + core}
    )

    @pl.when(row != colchip)
    def _():
        for h in range(2):
            pl.semaphore_signal(bar, inc=1, device_id=partner(h))

    me_x = x_hi * 2 + x_lo
    relay_row = x_lo * 4 + colchip % 4
    relay_chip = (row // 2) * 2 + x_hi
    to_x = (row % 2) * 2 + colchip // 4
    hop_x = (to_x - me_x + 4) % 4
    by_relay = (hop_x != 0) & ((relay_row != row) | (relay_chip != colchip))

    def source(k):
        xx = (me_x + k) % 4
        y_s = (z % 2) * 2 + xx // 2
        z_s = (xx % 2) * 2 + y // 2
        there = (x_hi == y % 2) & (x_lo == z // 2) & ((y_s != y) | (z_s != z))
        return x_lo * 4 + y_s, z_s * 2 + x_hi, there

    for k in range(1, 4):
        row_s, chip_s, there = source(k)

        @pl.when(there)
        def _():
            for h in range(2):
                pl.semaphore_signal(bar, inc=1, device_id={"row": row_s, "col": chip_s * 2 + h})

    def stage(o):
        v = slab[:, o, :]
        for k in range(4):
            send_l[o, k, :, 0:256] = v[:, k * 256 : k * 256 + 256]
            send_l[o, k, :, 256:512] = v[:, 1024 + k * 256 : 1280 + k * 256]
        w = slab[:, 3 - o, :]
        for k in range(4):
            for c in range(2):
                for h in range(2):
                    b = k * 512 + h * 256 + c * 128
                    send_r[o, k, :, c * 256 + h * 128 : c * 256 + h * 128 + 128] = w[:, b : b + 128]
        left[o, z, y] = send_l[o, y]
        right[o, y, z] = send_r[o, z]

    for cp in inputs:
        cp.wait()
    stage(0)
    pl.semaphore_wait(bar, 23 + jnp.where(row == colchip, 0, 2) + jnp.where(by_relay, 2, 0))

    def copy(src, dst, ssem, rsem, to):
        cp = pltpu.make_async_remote_copy(src, dst, ssem, rsem, device_id=to)
        cp.start()
        return cp

    def took(sem, like):
        pltpu.make_async_copy(like, like, sem).wait()

    scatter, gather = {}, {}

    def post_scatter(o):
        for d in (1, 3, 2):
            ky, kz = (y + d) % 4, (z + d) % 4
            scatter[o, 0, d] = copy(
                send_l.at[o, ky], left.at[o, z, y], a_s, a_r.at[0, o, d - 1], at_y(d)
            )
            scatter[o, 1, d] = copy(
                send_r.at[o, kz], right.at[o, y, z], a_s, a_r.at[1, o, d - 1], at_z(d)
            )

    def post_gather(o, d):
        ky, kz = (y - d) % 4, (z - d) % 4
        for way, step in ((0, 1), (1, 3)):
            sems = [g_r.at[side, o, d] if way == d % 2 else u_r.at[side, o] for side in range(2)]
            gather[o, 0, way, d] = copy(left.at[o, z, ky], left.at[o, z, ky], g_s, sems[0], at_z(step))
            gather[o, 1, way, d] = copy(right.at[o, y, kz], right.at[o, y, kz], g_s, sems[1], at_y(step))

    def rest_gather(o):
        for d in (1, 3, 2):
            scatter[o, 0, d].wait_recv()
            scatter[o, 1, d].wait_recv()
            post_gather(o, d)

    def forward(o, d):
        way, step = (0, 1) if d % 2 == 0 else (1, 3)
        kz, ky = (z - step) % 4, (y - step) % 4
        jy, jz = (y - d) % 4, (z - d) % 4
        gather[o, 0, way, d].wait_recv()
        copy(left.at[o, kz, jy], left.at[o, kz, jy], f_s, u_r.at[0, o], at_z(step))
        gather[o, 1, way, d].wait_recv()
        copy(right.at[o, ky, jz], right.at[o, ky, jz], f_s, u_r.at[1, o], at_y(step))

    def prepare(o):
        took(u_r.at[0, o], left.at[o, 0:2])
        took(u_r.at[1, o], right.at[o, 0:2])
        for k in range(4):
            v = left[o, k].reshape(128, 512).T
            hi = v.astype(BF16)
            lt_hi[o, :, k * 128 : k * 128 + 128] = hi
            lt_lo[o, :, k * 128 : k * 128 + 128] = (v - hi.astype(F32)).astype(BF16)
        for kz in range(4):
            for ky in range(4):
                w = right[o, ky, kz]
                hi = w.astype(BF16)
                lo = (w - hi.astype(F32)).astype(BF16)
                q = kz * 128 + ky * 32
                for h in range(2):
                    r_hi[o, h, q : q + 32, :] = hi[:, h * 256 : h * 256 + 256]
                    r_lo[o, h, q : q + 32, :] = lo[:, h * 256 : h * 256 + 256]

    def multiply(s, which, half):
        lo_, ro_, _ = SEQ[s]

        @pl.loop(0, 2)
        def _(ab):
            rows = pl.ds(pl.multiple_of(ab * 256, 256), 256)
            hi = lt_hi[lo_, rows, :]
            acc = jnp.dot(hi, r_hi[ro_, half], preferred_element_type=F32)
            acc += jnp.dot(hi, r_lo[ro_, half], preferred_element_type=F32)
            acc += jnp.dot(lt_lo[lo_, rows, :], r_hi[ro_, half], preferred_element_type=F32)
            part[s, which, ab] = acc[:, 0:128]
            part[s, which, 2 + ab] = acc[:, 128:256]

    exchanged, along_x = {}, {}

    def compute(s):
        multiply(s, 0, 1 - core)
        exchanged[s] = copy(part.at[s, 0], part_in.at[s], d_s, d_r.at[s], sibling)
        multiply(s, 1, core)

    up_x, down_x, far_x = (me_x + 1) % 4, (me_x + 3) % 4, (me_x + 2) % 4
    low, high = pl.ds(0, 128), pl.ds(128, 128)

    def reduce(s):
        exchanged[s].wait_recv()
        part[s, 1] = part[s, 1] + part_in[s]
        mine = part.at[s, 1]
        along_x[s, 0] = copy(mine.at[far_x, low], x_via.at[s, 0], x_s, x_r.at[s, 0], at_x(1))
        along_x[s, 1] = copy(mine.at[far_x, high], x_via.at[s, 1], x_s, x_r.at[s, 1], at_x(3))
        copy(mine.at[up_x, high], x_in.at[s, 0, high], x_s, x_r.at[s, 2], at_x(1))
        copy(mine.at[down_x, low], x_in.at[s, 1, low], x_s, x_r.at[s, 2], at_x(3))

    def reduce_on(s):
        mine = part.at[s, 1]
        along_x[s, 0].wait_recv()
        part[s, 1, up_x, 0:128] = part[s, 1, up_x, 0:128] + x_via[s, 0]
        copy(mine.at[up_x, low], x_in.at[s, 0, low], x_s, x_r.at[s, 2], at_x(1))
        along_x[s, 1].wait_recv()
        part[s, 1, down_x, 128:256] = part[s, 1, down_x, 128:256] + x_via[s, 1]
        copy(mine.at[down_x, high], x_in.at[s, 1, high], x_s, x_r.at[s, 2], at_x(3))

    def swap(s, h, part_no):
        rows = pl.ds(pl.multiple_of(h * 128 + part_no * 64, 64), 64)
        return pltpu.make_async_remote_copy(
            dfin.at[s, rows], t_in.at[s, core, pl.ds(part_no * 64, 64)],
            t_s.at[s], t_r.at[s], device_id=partner(h),
        )

    def swap_by_relay(s, h):
        rows = pl.ds(pl.multiple_of(h * 128 + 64, 64), 64)
        return pltpu.make_async_remote_copy(
            dfin.at[s, rows], via.at[s, hop_x - 1, core], t_s.at[s], v_r.at[s, hop_x - 1],
            device_id={"row": relay_row, "col": relay_chip * 2 + h},
        )

    def onto(s, k, c):
        row_s, chip_s, _ = source(k)
        return pltpu.make_async_remote_copy(
            via.at[s, k - 1, c], t_in.at[s, c, pl.ds(64, 64)], v_s.at[s, k - 1], t_r.at[s],
            device_id={"row": chip_s, "col": row_s * 2 + core},
        )

    def relays(s, k):
        row_s, chip_s, there = source(k)
        return there & (row_s < chip_s if s % 2 == 0 else row_s > chip_s)

    def relay(s):
        for k in range(1, 4):

            @pl.when(relays(s, k))
            def _():
                took(v_r.at[s, k - 1], via.at[s, k - 1])
                for c in range(2):
                    onto(s, k, c).start()

    def swap_sibling(s):
        return pltpu.make_async_remote_copy(
            dfin.at[s, pl.ds(pl.multiple_of((1 - core) * 128, 128), 128)], t_in.at[s, core],
            t_s.at[s], t_r.at[s], device_id=sibling,
        )

    def sends(s):
        return row < colchip if s % 2 == 0 else row > colchip

    def receives(s):
        return row > colchip if s % 2 == 0 else row < colchip

    written = []
    vir_b = vir[pl.ds(col, 1), :]

    def finish(s):
        took(x_r.at[s, 2], x_in.at[s])
        p = SEQ[s][2]
        i, j = PAIRS[p]
        total = part[s, 1, me_x] + (x_in[s, 0] + x_in[s, 1])
        dfin[s] = total

        amp = total / (((occ[i] + occ[j]) - vir_a[...]) - vir_b)
        amps[p] = amp
        written.append(pltpu.make_async_copy(amps.at[p], amps_hbm.at[p], o_s.at[p]))
        written[-1].start()
        e_acc[p] = jnp.sum((2.0 * (amp * total)).reshape(32, 8, 128), axis=0)

    def swap_start(s):
        @pl.when(sends(s))
        def _():
            for h in range(2):
                swap(s, h, 0).start()

        @pl.when(sends(s) & by_relay)
        def _():
            for h in range(2):
                swap_by_relay(s, h).start()

        @pl.when(sends(s) & jnp.logical_not(by_relay))
        def _():
            for h in range(2):
                swap(s, h, 1).start()

        @pl.when(row == colchip)
        def _():
            swap_sibling(s).start()
            t_in[s, core] = dfin[s, pl.ds(pl.multiple_of(core * 128, 128), 128), :]

    def swap_sent(s):
        @pl.when(sends(s))
        def _():
            took(t_s.at[s], dfin.at[s])

        @pl.when(row == colchip)
        def _():
            took(t_s.at[s], t_in.at[s, 0])

        for k in range(1, 4):

            @pl.when(relays(s, k))
            def _():
                took(v_s.at[s, k - 1], via.at[s, k - 1])

    def energy_swapped(s, weight):
        p = SEQ[s][2]
        prod = amps[p, 0:128] * t_in[s, 0].T + amps[p, 128:256] * t_in[s, 1].T
        e_acc[p] = e_acc[p] - weight * jnp.sum(prod.reshape(16, 8, 128), axis=0)

    def swapped(s):
        @pl.when(receives(s))
        def _():
            took(t_r.at[s], t_in.at[s])
            energy_swapped(s, 2.0)

        @pl.when(row == colchip)
        def _():
            took(t_r.at[s], t_in.at[s, 1 - core])
            energy_swapped(s, 1.0)

    def forward_rest(o):
        for d in (1, 3, 2):
            forward(o, d)

    post_scatter(0)
    post_gather(0, 0)
    stage(1)
    rest_gather(0)
    forward(0, 0)
    post_scatter(1)
    stage(2)
    for h in range(2):
        vir_a[h * 128 : h * 128 + 128, :] = jnp.broadcast_to(vir[pl.ds(row * 2 + h, 1), :], (128, 128)).T
    forward_rest(0)
    post_gather(1, 0)
    rest_gather(1)
    forward(1, 0)
    post_scatter(2)
    prepare(0)
    compute(0)
    reduce(0)
    forward_rest(1)
    post_gather(2, 0)
    reduce_on(0)
    rest_gather(2)
    forward(2, 0)
    finish(0)
    prepare(1)
    compute(1)
    compute(2)
    reduce(1)
    compute(3)
    reduce(2)
    reduce(3)
    forward_rest(2)
    swap_start(0)
    reduce_on(1)
    prepare(2)
    compute(4)
    reduce_on(2)
    compute(5)
    reduce(4)
    reduce_on(3)
    reduce(5)
    relay(0)
    finish(1)
    swap_start(1)
    finish(2)
    reduce_on(4)
    swap_start(2)
    relay(1)
    reduce_on(5)
    finish(3)
    swap_start(3)
    relay(2)
    relay(3)
    finish(4)
    swap_start(4)
    finish(5)
    swap_start(5)
    for s in range(4):
        swapped(s)
    relay(4)
    relay(5)
    swapped(4)
    swapped(5)

    e_tile = jnp.concatenate(
        [jnp.sum(e_acc[p], axis=0, keepdims=True) for p in range(6)] + [jnp.zeros((2, 128), F32)], axis=0
    )
    e_col[col] = e_tile
    for d in range(1, 16):
        copy(e_col.at[col], e_col.at[col], e1_s, e1_r, {"col": (col + d) % 16})
    took(a_s, left.at[:, 0:3, 0:2])
    took(g_s, left)
    took(f_s, left.at[:, 0:2])
    took(d_s, part_in)
    took(x_s, part.at[:, 0, 0:3])
    for s in range(6):
        swap_sent(s)
    took(e1_r, e_col.at[0:15])
    e_row[row] = jnp.sum(e_col[...], axis=0)
    for d in range(1, 8):
        copy(e_row.at[row], e_row.at[row], e2_s, e2_r, {"row": (row + d) % 8})
    took(e1_s, e_col.at[0:15])
    took(e2_r, e_row.at[0:7])
    whole = jnp.sum(e_row[...], axis=0)
    for p in range(6):
        energy[p] = jnp.sum(whole[p : p + 1]) * (2.0 / (NV * NV))
    took(e2_s, e_row.at[0:7])
    for cp in written:
        cp.wait()


def local(slab, occ_energy, vir_energy):
    dma = pltpu.SemaphoreType.DMA
    vmem = pltpu.VMEM
    amps, energy = pl.pallas_call(
        kernel,
        out_shape=(
            jax.ShapeDtypeStruct((6, 256, 128), F32),
            jax.ShapeDtypeStruct((6,), F32),
        ),
        in_specs=[pl.BlockSpec(memory_space=pltpu.HBM)] * 3,
        out_specs=(pl.BlockSpec(memory_space=pltpu.HBM), pl.BlockSpec(memory_space=pltpu.SMEM)),
        scratch_shapes=[
            vmem((NQ, 4, NV), F32),
            pltpu.SMEM((4,), F32),
            vmem((16, 128), F32),
            vmem((6, 256, 128), F32),
            vmem((3, 4, NQ, 512), F32),
            vmem((3, 4, NQ, 512), F32),
            vmem((3, 4, 4, NQ, 512), F32),
            vmem((3, 4, 4, NQ, 512), F32),
            vmem((3, 512, 512), BF16),
            vmem((3, 512, 512), BF16),
            vmem((3, 2, 512, 256), BF16),
            vmem((3, 2, 512, 256), BF16),
            vmem((6, 2, 4, 256, 128), F32),
            vmem((6, 4, 256, 128), F32),
            vmem((6, 2, 256, 128), F32),
            vmem((6, 2, 128, 128), F32),
            vmem((6, 256, 128), F32),
            vmem((6, 2, 128, 128), F32),
            vmem((6, 3, 2, 64, 128), F32),
            vmem((256, 128), F32),
            vmem((6, 8, 128), F32),
            vmem((16, 8, 128), F32),
            vmem((8, 8, 128), F32),
            dma,
            dma((2, 3, 3)),
            dma,
            dma((2, 3, 4)),
            dma((2, 3)),
            dma,
            dma,
            dma((6,)),
            dma,
            dma((6, 3)),
            dma((6,)),
            dma((6,)),
            dma((6, 3)),
            dma((6, 3)),
            dma,
            dma,
            dma,
            dma,
            dma((3,)),
            dma((6,)),
        ],
        compiler_params=pltpu.CompilerParams(
            collective_id=0, has_side_effects=True, vmem_limit_bytes=60 * 2**20
        ),
        name="pairs",
    )(slab, occ_energy, vir_energy.reshape(16, 128))
    return amps, energy


def solution(mesh):
    return jax.shard_map(
        local,
        mesh=mesh,
        in_specs=(P(("row", "col"), None, None), P(), P()),
        out_specs=(P(None, "row", "col"), P()),
        check_vma=False,
    )
```

```python
import jax
import jax.numpy as jnp
from jax import lax
from jax.experimental import pallas as pl
from jax.experimental.pallas import tpu as pltpu
from jax.sharding import PartitionSpec as P

F32, BF16 = jnp.float32, jnp.bfloat16
NQ = 32
NV = 2048
SEQ = [(0, 0, 2), (0, 1, 1), (1, 0, 4), (1, 1, 3), (0, 2, 0), (2, 0, 5)]
PAIRS = [(0, 1), (0, 2), (0, 3), (1, 2), (1, 3), (2, 3)]


def kernel(
    slab_hbm, occ_hbm, vir_hbm, amps_hbm, energy,
    slab, occ, vir, amps,
    send_l, send_r, left, right, lt_hi, lt_lo, r_hi, r_lo,
    part, part_in, x_in, x_via, dfin, t_in, via, vir_a, e_acc, e_col, e_row,
    a_s, a_r, g_s, g_r, u_r, f_s, d_s, d_r, x_s, x_r, t_s, t_r, v_s, v_r, e1_s, e1_r, e2_s, e2_r, i_s, o_s,
):
    row = lax.axis_index("row")
    col = lax.axis_index("col")
    x_lo, y = row // 4, row % 4
    z, x_hi, core = col // 4, (col // 2) % 2, col % 2
    colchip = col // 2

    def at_y(d):
        return {"row": x_lo * 4 + (y + d) % 4}

    def at_z(d):
        return {"col": ((z + d) % 4) * 4 + x_hi * 2 + core}

    def at_x(d):
        xx = (x_hi * 2 + x_lo + d) % 4
        return {"row": (xx % 2) * 4 + y, "col": (z * 2 + xx // 2) * 2 + core}

    sibling = {"col": colchip * 2 + 1 - core}

    def partner(h):
        return {"row": colchip, "col": row * 2 + h}

    inputs = [
        pltpu.make_async_copy(src, dst, i_s.at[n])
        for n, (src, dst) in enumerate([(slab_hbm, slab), (occ_hbm, occ), (vir_hbm, vir)])
    ]
    for cp in inputs:
        cp.start()
    bar = pltpu.get_barrier_semaphore()
    for d in range(1, 8):
        pl.semaphore_signal(bar, inc=1, device_id={"row": (row + d) % 8})
    for d in range(1, 16):
        pl.semaphore_signal(bar, inc=1, device_id={"col": (col + d) % 16})
    pl.semaphore_signal(
        bar, inc=1, device_id={"row": (1 - x_lo) * 4 + y, "col": (z * 2 + 1 - x_hi) * 2 + core}
    )

    @pl.when(row != colchip)
    def _():
        for h in range(2):
            pl.semaphore_signal(bar, inc=1, device_id=partner(h))

    me_x = x_hi * 2 + x_lo
    relay_row = x_lo * 4 + colchip % 4
    relay_chip = (row // 2) * 2 + x_hi
    to_x = (row % 2) * 2 + colchip // 4
    hop_x = (to_x - me_x + 4) % 4
    by_relay = (hop_x != 0) & ((relay_row != row) | (relay_chip != colchip))

    def source(k):
        xx = (me_x + k) % 4
        y_s = (z % 2) * 2 + xx // 2
        z_s = (xx % 2) * 2 + y // 2
        there = (x_hi == y % 2) & (x_lo == z // 2) & ((y_s != y) | (z_s != z))
        return x_lo * 4 + y_s, z_s * 2 + x_hi, there

    for k in range(1, 4):
        row_s, chip_s, there = source(k)

        @pl.when(there)
        def _():
            for h in range(2):
                pl.semaphore_signal(bar, inc=1, device_id={"row": row_s, "col": chip_s * 2 + h})

    def stage(o):
        v = slab[:, o, :]
        for k in range(4):
            send_l[o, k, :, 0:256] = v[:, k * 256 : k * 256 + 256]
            send_l[o, k, :, 256:512] = v[:, 1024 + k * 256 : 1280 + k * 256]
        w = slab[:, 3 - o, :]
        for k in range(4):
            for c in range(2):
                for h in range(2):
                    b = k * 512 + h * 256 + c * 128
                    send_r[o, k, :, c * 256 + h * 128 : c * 256 + h * 128 + 128] = w[:, b : b + 128]
        left[o, z, y] = send_l[o, y]
        right[o, y, z] = send_r[o, z]

    for cp in inputs:
        cp.wait()
    stage(0)
    pl.semaphore_wait(bar, 23 + jnp.where(row == colchip, 0, 2) + jnp.where(by_relay, 2, 0))

    def copy(src, dst, ssem, rsem, to):
        cp = pltpu.make_async_remote_copy(src, dst, ssem, rsem, device_id=to)
        cp.start()
        return cp

    def took(sem, like):
        pltpu.make_async_copy(like, like, sem).wait()

    scatter, gather = {}, {}

    def post_scatter(o):
        for d in (1, 3, 2):
            ky, kz = (y + d) % 4, (z + d) % 4
            scatter[o, 0, d] = copy(
                send_l.at[o, ky], left.at[o, z, y], a_s, a_r.at[0, o, d - 1], at_y(d)
            )
            scatter[o, 1, d] = copy(
                send_r.at[o, kz], right.at[o, y, z], a_s, a_r.at[1, o, d - 1], at_z(d)
            )

    def post_gather(o, d):
        ky, kz = (y - d) % 4, (z - d) % 4
        for way, step in ((0, 1), (1, 3)):
            sems = [g_r.at[side, o, d] if way == d % 2 else u_r.at[side, o] for side in range(2)]
            gather[o, 0, way, d] = copy(left.at[o, z, ky], left.at[o, z, ky], g_s, sems[0], at_z(step))
            gather[o, 1, way, d] = copy(right.at[o, y, kz], right.at[o, y, kz], g_s, sems[1], at_y(step))

    def rest_gather(o):
        for d in (1, 3, 2):
            scatter[o, 0, d].wait_recv()
            scatter[o, 1, d].wait_recv()
            post_gather(o, d)

    def forward(o, d):
        way, step = (0, 1) if d % 2 == 0 else (1, 3)
        kz, ky = (z - step) % 4, (y - step) % 4
        jy, jz = (y - d) % 4, (z - d) % 4
        gather[o, 0, way, d].wait_recv()
        copy(left.at[o, kz, jy], left.at[o, kz, jy], f_s, u_r.at[0, o], at_z(step))
        gather[o, 1, way, d].wait_recv()
        copy(right.at[o, ky, jz], right.at[o, ky, jz], f_s, u_r.at[1, o], at_y(step))

    def prepare(o):
        took(u_r.at[0, o], left.at[o, 0:2])
        took(u_r.at[1, o], right.at[o, 0:2])
        for k in range(4):
            v = left[o, k].reshape(128, 512).T
            hi = v.astype(BF16)
            lt_hi[o, :, k * 128 : k * 128 + 128] = hi
            lt_lo[o, :, k * 128 : k * 128 + 128] = (v - hi.astype(F32)).astype(BF16)
        for kz in range(4):
            for ky in range(4):
                w = right[o, ky, kz]
                hi = w.astype(BF16)
                lo = (w - hi.astype(F32)).astype(BF16)
                q = kz * 128 + ky * 32
                for h in range(2):
                    r_hi[o, h, q : q + 32, :] = hi[:, h * 256 : h * 256 + 256]
                    r_lo[o, h, q : q + 32, :] = lo[:, h * 256 : h * 256 + 256]

    def multiply(s, which, half):
        lo_, ro_, _ = SEQ[s]

        @pl.loop(0, 2)
        def _(ab):
            rows = pl.ds(pl.multiple_of(ab * 256, 256), 256)
            hi = lt_hi[lo_, rows, :]
            acc = jnp.dot(hi, r_hi[ro_, half], preferred_element_type=F32)
            acc += jnp.dot(hi, r_lo[ro_, half], preferred_element_type=F32)
            acc += jnp.dot(lt_lo[lo_, rows, :], r_hi[ro_, half], preferred_element_type=F32)
            part[s, which, ab] = acc[:, 0:128]
            part[s, which, 2 + ab] = acc[:, 128:256]

    exchanged, along_x = {}, {}

    def compute(s):
        multiply(s, 0, 1 - core)
        exchanged[s] = copy(part.at[s, 0], part_in.at[s], d_s, d_r.at[s], sibling)
        multiply(s, 1, core)

    up_x, down_x, far_x = (me_x + 1) % 4, (me_x + 3) % 4, (me_x + 2) % 4
    low, high = pl.ds(0, 128), pl.ds(128, 128)

    def reduce(s):
        exchanged[s].wait_recv()
        part[s, 1] = part[s, 1] + part_in[s]
        mine = part.at[s, 1]
        along_x[s, 0] = copy(mine.at[far_x, low], x_via.at[s, 0], x_s, x_r.at[s, 0], at_x(1))
        along_x[s, 1] = copy(mine.at[far_x, high], x_via.at[s, 1], x_s, x_r.at[s, 1], at_x(3))
        copy(mine.at[up_x, high], x_in.at[s, 0, high], x_s, x_r.at[s, 2], at_x(1))
        copy(mine.at[down_x, low], x_in.at[s, 1, low], x_s, x_r.at[s, 2], at_x(3))

    def reduce_on(s):
        mine = part.at[s, 1]
        along_x[s, 0].wait_recv()
        part[s, 1, up_x, 0:128] = part[s, 1, up_x, 0:128] + x_via[s, 0]
        copy(mine.at[up_x, low], x_in.at[s, 0, low], x_s, x_r.at[s, 2], at_x(1))
        along_x[s, 1].wait_recv()
        part[s, 1, down_x, 128:256] = part[s, 1, down_x, 128:256] + x_via[s, 1]
        copy(mine.at[down_x, high], x_in.at[s, 1, high], x_s, x_r.at[s, 2], at_x(3))

    def swap(s, h, part_no):
        rows = pl.ds(pl.multiple_of(h * 128 + part_no * 64, 64), 64)
        return pltpu.make_async_remote_copy(
            dfin.at[s, rows], t_in.at[s, core, pl.ds(part_no * 64, 64)],
            t_s.at[s], t_r.at[s], device_id=partner(h),
        )

    def swap_by_relay(s, h):
        rows = pl.ds(pl.multiple_of(h * 128 + 64, 64), 64)
        return pltpu.make_async_remote_copy(
            dfin.at[s, rows], via.at[s, hop_x - 1, core], t_s.at[s], v_r.at[s, hop_x - 1],
            device_id={"row": relay_row, "col": relay_chip * 2 + h},
        )

    def onto(s, k, c):
        row_s, chip_s, _ = source(k)
        return pltpu.make_async_remote_copy(
            via.at[s, k - 1, c], t_in.at[s, c, pl.ds(64, 64)], v_s.at[s, k - 1], t_r.at[s],
            device_id={"row": chip_s, "col": row_s * 2 + core},
        )

    def relays(s, k):
        row_s, chip_s, there = source(k)
        return there & (row_s < chip_s if s % 2 == 0 else row_s > chip_s)

    def relay(s):
        for k in range(1, 4):

            @pl.when(relays(s, k))
            def _():
                took(v_r.at[s, k - 1], via.at[s, k - 1])
                for c in range(2):
                    onto(s, k, c).start()

    def swap_sibling(s):
        return pltpu.make_async_remote_copy(
            dfin.at[s, pl.ds(pl.multiple_of((1 - core) * 128, 128), 128)], t_in.at[s, core],
            t_s.at[s], t_r.at[s], device_id=sibling,
        )

    def sends(s):
        return row < colchip if s % 2 == 0 else row > colchip

    def receives(s):
        return row > colchip if s % 2 == 0 else row < colchip

    written = []
    vir_b = vir[pl.ds(col, 1), :]

    def finish(s):
        took(x_r.at[s, 2], x_in.at[s])
        p = SEQ[s][2]
        i, j = PAIRS[p]
        total = part[s, 1, me_x] + (x_in[s, 0] + x_in[s, 1])
        dfin[s] = total

        amp = total / (((occ[i] + occ[j]) - vir_a[...]) - vir_b)
        amps[p] = amp
        written.append(pltpu.make_async_copy(amps.at[p], amps_hbm.at[p], o_s.at[p]))
        written[-1].start()
        e_acc[p] = jnp.sum((2.0 * (amp * total)).reshape(32, 8, 128), axis=0)

    def swap_start(s):
        @pl.when(sends(s))
        def _():
            for h in range(2):
                swap(s, h, 0).start()

        @pl.when(sends(s) & by_relay)
        def _():
            for h in range(2):
                swap_by_relay(s, h).start()

        @pl.when(sends(s) & jnp.logical_not(by_relay))
        def _():
            for h in range(2):
                swap(s, h, 1).start()

        @pl.when(row == colchip)
        def _():
            swap_sibling(s).start()
            t_in[s, core] = dfin[s, pl.ds(pl.multiple_of(core * 128, 128), 128), :]

    def swap_sent(s):
        @pl.when(sends(s))
        def _():
            took(t_s.at[s], dfin.at[s])

        @pl.when(row == colchip)
        def _():
            took(t_s.at[s], t_in.at[s, 0])

        for k in range(1, 4):

            @pl.when(relays(s, k))
            def _():
                took(v_s.at[s, k - 1], via.at[s, k - 1])

    def energy_swapped(s, weight):
        p = SEQ[s][2]
        prod = amps[p, 0:128] * t_in[s, 0].T + amps[p, 128:256] * t_in[s, 1].T
        e_acc[p] = e_acc[p] - weight * jnp.sum(prod.reshape(16, 8, 128), axis=0)

    def swapped(s):
        @pl.when(receives(s))
        def _():
            took(t_r.at[s], t_in.at[s])
            energy_swapped(s, 2.0)

        @pl.when(row == colchip)
        def _():
            took(t_r.at[s], t_in.at[s, 1 - core])
            energy_swapped(s, 1.0)

    def forward_rest(o):
        for d in (1, 3, 2):
            forward(o, d)

    post_scatter(0)
    post_gather(0, 0)
    stage(1)
    rest_gather(0)
    forward(0, 0)
    post_scatter(1)
    stage(2)
    for h in range(2):
        vir_a[h * 128 : h * 128 + 128, :] = jnp.broadcast_to(vir[pl.ds(row * 2 + h, 1), :], (128, 128)).T
    forward_rest(0)
    post_gather(1, 0)
    rest_gather(1)
    forward(1, 0)
    prepare(0)
    compute(0)
    reduce(0)
    forward_rest(1)
    post_scatter(2)
    post_gather(2, 0)
    reduce_on(0)
    rest_gather(2)
    forward(2, 0)
    finish(0)
    prepare(1)
    compute(1)
    compute(2)
    reduce(1)
    compute(3)
    reduce(2)
    reduce(3)
    forward_rest(2)
    swap_start(0)
    reduce_on(1)
    prepare(2)
    compute(4)
    reduce_on(2)
    compute(5)
    reduce(4)
    reduce_on(3)
    reduce(5)
    relay(0)
    finish(1)
    swap_start(1)
    finish(2)
    reduce_on(4)
    swap_start(2)
    relay(1)
    reduce_on(5)
    finish(3)
    swap_start(3)
    relay(2)
    relay(3)
    finish(4)
    swap_start(4)
    finish(5)
    swap_start(5)
    for s in range(4):
        swapped(s)
    relay(4)
    relay(5)
    swapped(4)
    swapped(5)

    e_tile = jnp.concatenate(
        [jnp.sum(e_acc[p], axis=0, keepdims=True) for p in range(6)] + [jnp.zeros((2, 128), F32)], axis=0
    )
    e_col[col] = e_tile
    for d in range(1, 16):
        copy(e_col.at[col], e_col.at[col], e1_s, e1_r, {"col": (col + d) % 16})
    took(a_s, left.at[:, 0:3, 0:2])
    took(g_s, left)
    took(f_s, left.at[:, 0:2])
    took(d_s, part_in)
    took(x_s, part.at[:, 0, 0:3])
    for s in range(6):
        swap_sent(s)
    took(e1_r, e_col.at[0:15])
    e_row[row] = jnp.sum(e_col[...], axis=0)
    for d in range(1, 8):
        copy(e_row.at[row], e_row.at[row], e2_s, e2_r, {"row": (row + d) % 8})
    took(e1_s, e_col.at[0:15])
    took(e2_r, e_row.at[0:7])
    whole = jnp.sum(e_row[...], axis=0)
    for p in range(6):
        energy[p] = jnp.sum(whole[p : p + 1]) * (2.0 / (NV * NV))
    took(e2_s, e_row.at[0:7])
    for cp in written:
        cp.wait()


def local(slab, occ_energy, vir_energy):
    dma = pltpu.SemaphoreType.DMA
    vmem = pltpu.VMEM
    amps, energy = pl.pallas_call(
        kernel,
        out_shape=(
            jax.ShapeDtypeStruct((6, 256, 128), F32),
            jax.ShapeDtypeStruct((6,), F32),
        ),
        in_specs=[pl.BlockSpec(memory_space=pltpu.HBM)] * 3,
        out_specs=(pl.BlockSpec(memory_space=pltpu.HBM), pl.BlockSpec(memory_space=pltpu.SMEM)),
        scratch_shapes=[
            vmem((NQ, 4, NV), F32),
            pltpu.SMEM((4,), F32),
            vmem((16, 128), F32),
            vmem((6, 256, 128), F32),
            vmem((3, 4, NQ, 512), F32),
            vmem((3, 4, NQ, 512), F32),
            vmem((3, 4, 4, NQ, 512), F32),
            vmem((3, 4, 4, NQ, 512), F32),
            vmem((3, 512, 512), BF16),
            vmem((3, 512, 512), BF16),
            vmem((3, 2, 512, 256), BF16),
            vmem((3, 2, 512, 256), BF16),
            vmem((6, 2, 4, 256, 128), F32),
            vmem((6, 4, 256, 128), F32),
            vmem((6, 2, 256, 128), F32),
            vmem((6, 2, 128, 128), F32),
            vmem((6, 256, 128), F32),
            vmem((6, 2, 128, 128), F32),
            vmem((6, 3, 2, 64, 128), F32),
            vmem((256, 128), F32),
            vmem((6, 8, 128), F32),
            vmem((16, 8, 128), F32),
            vmem((8, 8, 128), F32),
            dma,
            dma((2, 3, 3)),
            dma,
            dma((2, 3, 4)),
            dma((2, 3)),
            dma,
            dma,
            dma((6,)),
            dma,
            dma((6, 3)),
            dma((6,)),
            dma((6,)),
            dma((6, 3)),
            dma((6, 3)),
            dma,
            dma,
            dma,
            dma,
            dma((3,)),
            dma((6,)),
        ],
        compiler_params=pltpu.CompilerParams(
            collective_id=0, has_side_effects=True, vmem_limit_bytes=60 * 2**20
        ),
        name="pairs",
    )(slab, occ_energy, vir_energy.reshape(16, 128))
    return amps, energy


def solution(mesh):
    return jax.shard_map(
        local,
        mesh=mesh,
        in_specs=(P(("row", "col"), None, None), P(), P()),
        out_specs=(P(None, "row", "col"), P()),
        check_vma=False,
    )
```
